256 devices in a mesh: dp: 16 (over z, core), tensor: 16 (over x, y).
Axes of the slice: x: 4, y: 4, z: 8, core: 2. Of those that a mesh axis runs over, the one named last changes fastest.
Arguments:
- grad_gate: bfloat16 [16, 28672, 256], P('dp', 'tensor'), may hold values from -6 to 6
- error_gate: float32 [16, 28672, 256], P('dp', 'tensor'), may hold values from -4 to 4
- query_gate: float32 [32, 256], replicated, may hold values from -6 to 6
- grad_down: bfloat16 [16, 256, 28672], P('dp', None, 'tensor'), may hold values from -6 to 6
- error_down: float32 [16, 256, 28672], P('dp', None, 'tensor'), may hold values from -4 to 4
- query_down: float32 [32, 28672], P(None, 'tensor'), may hold values from -6 to 6
Outputs:
- update_gate: float32 [28672, 256], P('tensor')
- new_error_gate: float32 [16, 28672, 256], P('dp', 'tensor')
- update_down: float32 [256, 28672], P(None, 'tensor')
- new_error_down: float32 [16, 256, 28672], P('dp', None, 'tensor')
The draws below stay inside these ranges and needn't reach their ends.
All inputs are finite; a program needn't handle non-finite values.
Results may differ from the reference program's by a relative error of at most 0.0003.
Values sent between devices are 32-bit elements; how exact they have to be, the bound alone decides.
A program may use at most 64 MiB of HBM per device.

```python
import jax
import jax.numpy as jnp
from jax import lax

FF = 28672
ROWS = 256
RANK = 32
WORKERS = 16


def steps_of(rng, extent, shards, smallest, high):
    loudness = 1.0
    for position, shards_of in shards:
        steps = jax.random.uniform(jax.random.fold_in(jax.random.fold_in(rng, 6), position), (shards_of,), jnp.float32, smallest / len(shards), high / len(shards))
        loudness = loudness * jnp.repeat(jnp.exp(steps), extent[position] // shards_of).reshape((-1,) + (1,) * (len(extent) - 1 - position))
    return loudness


def normal_values(stream_key, shape, width, most, pieces=(), held_as=jnp.bfloat16):
    factor_of = steps_of(stream_key, shape, pieces, -0.22, 0.18) if pieces else 1.0
    array = jax.random.normal(stream_key, shape, jnp.float32) * width * factor_of
    return jnp.minimum(jnp.maximum(array, -most), most).astype(held_as)


def setup_inputs(seed: int = 0) -> dict:
    splits = jax.random.split(jax.random.key(seed), 7)
    grad_gate = normal_values(splits[0], (WORKERS, FF, ROWS), 1.0, 6.0, ((0, 16), (1, 16)))
    error_gate = normal_values(splits[1], (WORKERS, FF, ROWS), 0.5, 4.0, ((0, 16), (1, 16)), jnp.float32)
    query_gate = normal_values(splits[2], (RANK, ROWS), 1.0, 6.0, (), jnp.float32)
    grad_down = normal_values(splits[3], (WORKERS, ROWS, FF), 1.0, 6.0, ((0, 16), (2, 16)))
    error_down = normal_values(splits[4], (WORKERS, ROWS, FF), 0.5, 4.0, ((0, 16), (2, 16)), jnp.float32)
    query_down = normal_values(splits[5], (RANK, FF), 1.0, 6.0, ((1, 16),), jnp.float32)
    return dict(grad_gate=grad_gate, error_gate=error_gate, query_gate=query_gate, grad_down=grad_down, error_down=error_down, query_down=query_down)


HIGH = lax.Precision.HIGHEST

def orthonormal_rows(sketch):
    gram = jnp.dot(sketch, sketch.T, precision=HIGH)
    lower = jnp.linalg.cholesky(gram)
    return lax.linalg.triangular_solve(lower, sketch, left_side=True, lower=True)

def reference(grad_gate, error_gate, query_gate, grad_down, error_down, query_down):
    full_gate = grad_gate.astype(jnp.float32) + error_gate
    full_down = grad_down.astype(jnp.float32) + error_down
    sketch_gate = jnp.einsum('kr,wfr->kf', query_gate, full_gate, precision=HIGH)
    sketch_down = jnp.einsum('kf,wrf->kr', query_down, full_down, precision=HIGH)
    basis_gate = orthonormal_rows(sketch_gate)
    basis_down = orthonormal_rows(sketch_down)
    workers = full_gate.shape[0]
    coeff_gate = jnp.einsum('kf,wfr->kr', basis_gate, full_gate, precision=HIGH) / workers
    coeff_down = jnp.einsum('kr,wrf->kf', basis_down, full_down, precision=HIGH) / workers
    update_gate = jnp.dot(basis_gate.T, coeff_gate, precision=HIGH)
    update_down = jnp.dot(basis_down.T, coeff_down, precision=HIGH)
    return (update_gate, full_gate - update_gate[None], update_down, full_down - update_down[None])
```

```python
import functools

import jax
import jax.numpy as jnp
from jax import lax
from jax.experimental import pallas as pl
from jax.experimental.pallas import tpu as pltpu
from jax.sharding import PartitionSpec as P

MESH = pl.DeviceIdType.MESH
F32, BF16 = jnp.float32, jnp.bfloat16
HIGH = lax.Precision.HIGHEST
NN = (((1,), (0,)), ((), ()))
NT = (((1,), (1,)), ((), ()))
TN = (((0,), (0,)), ((), ()))
LANES = 128
BLOCK = 256
RANK = 32
Z, XY = 8, 16
OWNERS = 7
Z_ORDER = (4, 3, 5, 2, 6, 1, 7)
XY_ORDER = sorted(
    ((dx, dy) for dx in range(4) for dy in range(4) if dx or dy),
    key=lambda o: -(min(o[0], 4 - o[0]) + min(o[1], 4 - o[1])),
)


def split3(x):
    hi = x.astype(BF16)
    rest = x - hi.astype(F32)
    mid = rest.astype(BF16)
    return hi, mid, (rest - mid.astype(F32)).astype(BF16)


def rows3(x):
    return jnp.concatenate(split3(x), axis=0)


def dot(a, b, dims):
    return lax.dot_general(a, b, dims, preferred_element_type=F32)


def dot_high(a, b, dims):
    return lax.dot_general(a, b, dims, precision=HIGH, preferred_element_type=F32)


def dot6(left3, right, dims):
    hi, mid, lo = right
    a = dot(left3, hi, dims)
    b = dot(left3[: 2 * RANK], mid, dims)
    c = dot(left3[:RANK], lo, dims)
    small = a[2 * RANK :] + b[RANK:] + c
    return a[:RANK] + ((a[RANK : 2 * RANK] + b[:RANK]) + small)


def total(ref, n):
    out = ref[0]
    for i in range(1, n):
        out = out + ref[i]
    return out


def eliminate(gram):
    rows = lax.broadcasted_iota(jnp.int32, (RANK, LANES), 0)
    lanes = lax.broadcasted_iota(jnp.int32, (RANK, LANES), 1)
    a = gram + (lanes == rows + RANK).astype(F32)
    index = lax.broadcasted_iota(jnp.int32, (RANK, 1), 0)
    inverse = jnp.zeros((RANK, 1), F32)
    for k in range(RANK):
        row = a[k : k + 1, :]
        inv = 1.0 / a[k : k + 1, k : k + 1]
        inverse = jnp.where(index == k, inv, inverse)
        column = a[:, k : k + 1]
        a = a - jnp.where(index > k, column * inv, 0.0) * row
    return a[:, RANK : 2 * RANK], inverse


def exchange_kernel(
    gg_hbm, eg_hbm, qg_hbm, gd_hbm, ed_hbm, qd_hbm,
    basis_g, coeff_g, basis_d, coeff_d,
    gg, eg, qg, gd, ed, qd, fg, fd,
    sg_part, sg_sib, sg_half, rs_g, sg,
    sfg, sfg_sib, msg_g, z1_g, x1_g, mid_g, z2_g, x2_g, full_g,
    sd_part, sd_sib, msg_d, z1_d, x1_d, mid_d, z2_d, x2_d, sd,
    sfd, sfd_sib, sfd_half, rs_d, own_g, own_d,
    load_sem, send_sem, recv_sem,
):
    dp, t = lax.axis_index("dp"), lax.axis_index("tensor")
    z, c = dp // 2, dp % 2
    x, y = t // 4, t % 4
    sibling = (dp + 1 - 2 * c, t)
    z_peers = [(lax.rem(z + i, Z), (2 * lax.rem(z + i, Z) + c, t)) for i in Z_ORDER]
    xy_peers = [(dp, lax.rem(x + dx, 4) * 4 + lax.rem(y + dy, 4)) for dx, dy in XY_ORDER]

    barrier = pltpu.get_barrier_semaphore()
    for device in [sibling] + [d for _, d in z_peers] + xy_peers:
        pl.semaphore_signal(barrier, inc=1, device_id=device, device_id_type=MESH)

    loads = [
        pltpu.make_async_copy(src, dst, load_sem.at[i])
        for i, (src, dst) in enumerate(
            ((qd_hbm, qd), (gd_hbm, gd), (ed_hbm, ed), (qg_hbm, qg), (gg_hbm, gg), (eg_hbm, eg))
        )
    ]
    for load in loads:
        load.start()

    def send(stage, src, dst, device):
        pltpu.make_async_remote_copy(
            src_ref=src, dst_ref=dst, send_sem=send_sem.at[stage], recv_sem=recv_sem.at[stage],
            device_id=device, device_id_type=MESH,
        ).start()

    def received(stage, ref):
        pltpu.make_async_copy(ref, ref, recv_sem.at[stage]).wait()

    def sent(stage, ref):
        pltpu.make_async_copy(ref, ref, send_sem.at[stage]).wait()

    blocks = gg.shape[0] // BLOCK
    for load in loads[:3]:
        load.wait()
    sd_sum = None
    for b in range(blocks):
        cols = pl.ds(b * BLOCK, BLOCK)
        parts = split3(gd[:, cols].astype(F32) + ed[:, cols])
        for i in range(3):
            fd[i, :, cols] = parts[i]
        term = dot6(rows3(qd[:, cols]), parts, NT)
        sd_sum = term if sd_sum is None else sd_sum + term
    sd_part[0] = sd_sum[:, :LANES]
    sd_part[1] = sd_sum[:, LANES:]
    for load in loads[3:]:
        load.wait()
    qg3 = rows3(qg[...])
    for b in range(blocks):
        rows = pl.ds(b * BLOCK, BLOCK)
        parts = split3(gg[rows, :].astype(F32) + eg[rows, :])
        for i in range(3):
            fg[i, rows, :] = parts[i]
        term = dot6(qg3, parts, NT)
        sg_part[2 * b] = term[:, :LANES]
        sg_part[2 * b + 1] = term[:, LANES:]

    pl.semaphore_wait(barrier, 1 + len(z_peers) + len(xy_peers))

    mine, other = OWNERS * c, OWNERS * (1 - c)
    send(0, sd_part.at[1 - c], sd_sib, sibling)
    send(1, sg_part.at[pl.ds(other, OWNERS)], sg_sib, sibling)

    def reduce_first(base, value, extra, msg, z1, x1):
        msg[0:32] = value
        if extra is not None:
            msg[32:40] = extra
        z1[z] = msg[0:16]
        high = msg.at[pl.ds(16, msg.shape[0] - 16)]
        x1[t] = high[...]
        for device in xy_peers:
            send(base + 1, high, x1.at[t], device)
        for _, device in z_peers:
            send(base, msg.at[pl.ds(0, 16)], z1.at[z], device)

    def reduce_second(base, z1, x1, mid, z2, x2):
        received(base, z1.at[pl.ds(0, Z - 1)])
        low = total(z1, Z)
        mid[0:16] = low
        x2[t] = low
        for device in xy_peers:
            send(base + 3, mid.at[pl.ds(0, 16)], x2.at[t], device)
        received(base + 1, x1.at[pl.ds(0, XY - 1)])
        high = total(x1, XY)
        mid[16:32] = high[0:16]
        z2[z] = high[0:16]
        for _, device in z_peers:
            send(base + 2, mid.at[pl.ds(16, 16)], z2.at[z], device)
        return high[16:]

    def reduce_third(base, z2, x2, full):
        received(base + 2, z2.at[pl.ds(0, Z - 1)])
        received(base + 3, x2.at[pl.ds(0, XY - 1)])
        full[c, 0:16] = total(x2, XY)
        full[c, 16:32] = total(z2, Z)
        send(base + 4, full.at[c], full.at[c], sibling)

    def scatter(stage, half, rs):
        for peer, device in z_peers:
            @pl.when(peer < OWNERS)
            def _():
                send(stage, half.at[peer], rs.at[z], device)

        @pl.when(z < OWNERS)
        def _():
            rs[z] = half[z]

    def gather(stage, own, dst):
        @pl.when(z < OWNERS)
        def _():
            dst[mine + z] = own[...]
            for _, device in z_peers:
                send(stage, own, dst.at[mine + z], device)

    def gathered(stage, dst):
        @pl.when(z < OWNERS)
        def _():
            received(stage, dst.at[pl.ds(0, OWNERS - 1)])

        @pl.when(z == OWNERS)
        def _():
            received(stage, dst.at[pl.ds(0, OWNERS)])

    received(0, sd_sib)
    reduce_first(2, sd_part[c] + sd_sib[...], None, msg_d, z1_d, x1_d)
    received(1, sg_sib)
    for i in range(OWNERS):
        sg_half[i] = sg_part[mine + i] + sg_sib[i]
    scatter(7, sg_half, rs_g)

    reduce_second(2, z1_d, x1_d, mid_d, z2_d, x2_d)

    @pl.when(z < OWNERS)
    def _():
        received(7, rs_g.at[pl.ds(0, Z - 1)])
        own_g[...] = total(rs_g, Z)

    gather(8, own_g, sg)

    reduce_third(2, z2_d, x2_d, sd)
    received(6, sd.at[1 - c])

    sketch_d = jnp.concatenate([sd[0], sd[1]], axis=1)
    sd3 = rows3(sketch_d)
    for b in range(blocks):
        cols = pl.ds(b * BLOCK, BLOCK)
        term = dot6(sd3, [fd[i, :, cols] for i in range(3)], NN)
        sfd[2 * b] = term[:, :LANES]
        sfd[2 * b + 1] = term[:, LANES:]
    send(9, sfd.at[pl.ds(other, OWNERS)], sfd_sib, sibling)

    gathered(8, sg)
    send(10, sg.at[pl.ds(mine, OWNERS)], sg.at[pl.ds(mine, OWNERS)], sibling)
    received(9, sfd_sib)
    for i in range(OWNERS):
        sfd_half[i] = sfd[mine + i] + sfd_sib[i]
    scatter(11, sfd_half, rs_d)

    received(10, sg.at[pl.ds(other, OWNERS)])
    sfg_sum = None
    gram_sum = None
    zeros = jnp.zeros((LANES - RANK, BLOCK), F32)
    for b in range(blocks):
        rows = pl.ds(b * BLOCK, BLOCK)
        tile = jnp.concatenate([sg[2 * b], sg[2 * b + 1]], axis=1)
        term = dot6(rows3(tile), [fg[i, rows, :] for i in range(3)], NN)
        sfg_sum = term if sfg_sum is None else sfg_sum + term
        term = dot_high(tile, jnp.concatenate([tile, zeros], axis=0), NT)
        gram_sum = term if gram_sum is None else gram_sum + term
    packed = gram_sum[0:8]
    for i in range(1, 4):
        packed = packed + pltpu.roll(gram_sum[8 * i : 8 * i + 8], RANK * i, 1)
    sfg[0] = sfg_sum[:, :LANES]
    sfg[1] = sfg_sum[:, LANES:]
    send(12, sfg.at[1 - c], sfg_sib, sibling)

    pad = jnp.zeros((LANES - RANK, BLOCK), F32)
    lower_d, inv_d = eliminate(dot_high(sketch_d, jnp.concatenate([sketch_d, pad], axis=0), NT))
    basis_d[...] = dot_high(lower_d, sketch_d, NN)

    received(12, sfg_sib)
    reduce_first(13, sfg[c] + sfg_sib[...], packed, msg_g, z1_g, x1_g)

    @pl.when(z < OWNERS)
    def _():
        received(11, rs_d.at[pl.ds(0, Z - 1)])
        own_d[...] = dot_high(lower_d, total(rs_d, Z), NN) * (inv_d * (1.0 / 16.0))

    gather(18, own_d, coeff_d)

    gram_packed = reduce_second(13, z1_g, x1_g, mid_g, z2_g, x2_g)
    lane = lax.broadcasted_iota(jnp.int32, (8, LANES), 1)
    gram_g = jnp.concatenate(
        [jnp.where(lane < RANK, gram_packed if i == 0 else pltpu.roll(gram_packed, LANES - RANK * i, 1), 0.0) for i in range(4)],
        axis=0,
    )
    lower_g, inv_g = eliminate(gram_g)
    for i in range(2 * OWNERS):
        basis_g[i] = dot_high(lower_g, sg[i], NN)

    gathered(18, coeff_d)
    send(19, coeff_d.at[pl.ds(mine, OWNERS)], coeff_d.at[pl.ds(mine, OWNERS)], sibling)

    reduce_third(13, z2_g, x2_g, full_g)
    received(17, full_g.at[1 - c])
    coeff_g[...] = dot_high(lower_g, jnp.concatenate([full_g[0], full_g[1]], axis=1), NN) * (inv_g * (1.0 / 16.0))
    received(19, coeff_d.at[pl.ds(other, OWNERS)])

    sent(0, sd_sib)
    sent(1, sg_sib)
    sent(9, sfd_sib)
    sent(12, sfg_sib)
    sent(10, sg_sib)
    sent(19, sg_sib)
    for base, msg, z1, x1, z2, x2, full in (
        (2, msg_d, z1_d, x1_d, z2_d, x2_d, sd),
        (13, msg_g, z1_g, x1_g, z2_g, x2_g, full_g),
    ):
        sent(base, z1.at[pl.ds(0, Z - 1)])
        sent(base + 1, x1.at[pl.ds(0, XY - 1)])
        sent(base + 2, z2.at[pl.ds(0, Z - 1)])
        sent(base + 3, x2.at[pl.ds(0, XY - 1)])
        sent(base + 4, full.at[0])
    for scatter_stage, gather_stage, rs in ((7, 8, rs_g), (11, 18, rs_d)):
        @pl.when(z < OWNERS)
        def _():
            sent(scatter_stage, rs.at[pl.ds(0, OWNERS - 1)])
            sent(gather_stage, rs.at[pl.ds(0, Z - 1)])

        @pl.when(z == OWNERS)
        def _():
            sent(scatter_stage, rs.at[pl.ds(0, OWNERS)])


def finish_kernel(gg, eg, gd, ed, basis_g, coeff_g, basis_d, coeff_d, ug, ng, ud, nd):
    left = jnp.concatenate([basis_g[0], basis_g[1]], axis=1)
    update = dot_high(left, coeff_g[...], TN)
    ug[...] = update
    ng[...] = (gg[...].astype(F32) + eg[...]) - update
    right = jnp.concatenate([coeff_d[0], coeff_d[1]], axis=1)
    update = dot_high(basis_d[...], right, TN)
    ud[...] = update
    nd[...] = (gd[...].astype(F32) + ed[...]) - update


def local(grad_gate, error_gate, query_gate, grad_down, error_down, query_down):
    gg, eg, gd, ed = grad_gate[0], error_gate[0], grad_down[0], error_down[0]
    ff, rows = gg.shape
    tiles = ff // LANES
    vmem = pltpu.VMEM
    tile = (RANK, LANES)

    def stack(n, r=RANK):
        return vmem((n, r, LANES), F32)

    def reduce_buffers(extra):
        return [vmem((RANK + extra, LANES), F32), stack(Z, 16), stack(XY, 16 + extra), vmem(tile, F32), stack(Z, 16), stack(XY, 16), stack(2)]

    scratch = (
        [vmem((ff, rows), BF16), vmem((ff, rows), F32), vmem((RANK, rows), F32)]
        + [vmem((rows, ff), BF16), vmem((rows, ff), F32), vmem((RANK, ff), F32)]
        + [vmem((3, ff, rows), BF16), vmem((3, rows, ff), BF16)]
        + [stack(tiles), stack(OWNERS), stack(OWNERS), stack(Z), stack(tiles)]
        + [stack(2), vmem(tile, F32)] + reduce_buffers(8)
        + [stack(2), vmem(tile, F32)] + reduce_buffers(0)
        + [stack(tiles), stack(OWNERS), stack(OWNERS), stack(Z), vmem(tile, F32), vmem(tile, F32)]
        + [pltpu.SemaphoreType.DMA((6,)), pltpu.SemaphoreType.DMA((20,)), pltpu.SemaphoreType.DMA((20,))]
    )
    whole = pl.BlockSpec(memory_space=pltpu.VMEM)
    basis_g, coeff_g, basis_d, coeff_d = pl.pallas_call(
        exchange_kernel,
        out_shape=[
            jax.ShapeDtypeStruct((tiles, RANK, LANES), F32),
            jax.ShapeDtypeStruct((RANK, rows), F32),
            jax.ShapeDtypeStruct((RANK, rows), F32),
            jax.ShapeDtypeStruct((tiles, RANK, LANES), F32),
        ],
        in_specs=[pl.BlockSpec(memory_space=pl.ANY)] * 6,
        out_specs=[whole] * 4,
        scratch_shapes=scratch,
        compiler_params=pltpu.CompilerParams(collective_id=0, has_side_effects=True, vmem_limit_bytes=48 * 2**20),
    )(gg, eg, query_gate, gd, ed, query_down)

    gate = pl.BlockSpec((BLOCK, rows), lambda i: (i, 0))
    down = pl.BlockSpec((rows, BLOCK), lambda i: (0, i))
    small = pl.BlockSpec((RANK, rows), lambda i: (0, 0))
    pair = pl.BlockSpec((2, RANK, LANES), lambda i: (i, 0, 0))
    gate_shape = jax.ShapeDtypeStruct((ff, rows), F32)
    down_shape = jax.ShapeDtypeStruct((rows, ff), F32)
    ug, ng, ud, nd = pl.pallas_call(
        finish_kernel,
        grid=(ff // BLOCK,),
        out_shape=[gate_shape, gate_shape, down_shape, down_shape],
        in_specs=[gate, gate, down, down, pair, small, small, pair],
        out_specs=[gate, gate, down, down],
        compiler_params=pltpu.CompilerParams(vmem_limit_bytes=48 * 2**20),
    )(gg, eg, gd, ed, basis_g, coeff_g, basis_d, coeff_d)
    return ug, ng[None], ud, nd[None]


def solution(mesh):
    in_specs = (
        P("dp", "tensor", None),
        P("dp", "tensor", None),
        P(),
        P("dp", None, "tensor"),
        P("dp", None, "tensor"),
        P(None, "tensor"),
    )
    out_specs = (
        P("tensor", None),
        P("dp", "tensor", None),
        P(None, "tensor"),
        P("dp", None, "tensor"),
    )
    return jax.shard_map(local, mesh=mesh, in_specs=in_specs, out_specs=out_specs, check_vma=False)
```

```python
import functools

import jax
import jax.numpy as jnp
from jax import lax
from jax.experimental import pallas as pl
from jax.experimental.pallas import tpu as pltpu
from jax.sharding import PartitionSpec as P

MESH = pl.DeviceIdType.MESH
F32, BF16 = jnp.float32, jnp.bfloat16
HIGH = lax.Precision.HIGHEST
NN = (((1,), (0,)), ((), ()))
NT = (((1,), (1,)), ((), ()))
TN = (((0,), (0,)), ((), ()))
LANES = 128
BLOCK = 256
RANK = 32
Z, XY = 8, 16
OWNERS = 7
Z_ORDER = (4, 3, 5, 2, 6, 1, 7)
XY_ORDER = sorted(
    ((dx, dy) for dx in range(4) for dy in range(4) if dx or dy),
    key=lambda o: -(min(o[0], 4 - o[0]) + min(o[1], 4 - o[1])),
)


def split3(x):
    hi = x.astype(BF16)
    rest = x - hi.astype(F32)
    mid = rest.astype(BF16)
    return hi, mid, (rest - mid.astype(F32)).astype(BF16)


def rows3(x):
    return jnp.concatenate(split3(x), axis=0)


def dot(a, b, dims):
    return lax.dot_general(a, b, dims, preferred_element_type=F32)


def dot_high(a, b, dims):
    return lax.dot_general(a, b, dims, precision=HIGH, preferred_element_type=F32)


def dot6(left3, right, dims):
    hi, mid, lo = right
    a = dot(left3, hi, dims)
    b = dot(left3[: 2 * RANK], mid, dims)
    c = dot(left3[:RANK], lo, dims)
    small = a[2 * RANK :] + b[RANK:] + c
    return a[:RANK] + ((a[RANK : 2 * RANK] + b[:RANK]) + small)


def total(ref, n):
    out = ref[0]
    for i in range(1, n):
        out = out + ref[i]
    return out


def eliminate(gram):
    rows = lax.broadcasted_iota(jnp.int32, (RANK, LANES), 0)
    lanes = lax.broadcasted_iota(jnp.int32, (RANK, LANES), 1)
    a = gram + (lanes == rows + RANK).astype(F32)
    index = lax.broadcasted_iota(jnp.int32, (RANK, 1), 0)
    inverse = jnp.zeros((RANK, 1), F32)
    for k in range(RANK):
        row = a[k : k + 1, :]
        inv = 1.0 / a[k : k + 1, k : k + 1]
        inverse = jnp.where(index == k, inv, inverse)
        column = a[:, k : k + 1]
        a = a - jnp.where(index > k, column * inv, 0.0) * row
    return a[:, RANK : 2 * RANK], inverse


def left_six(x):
    hi, mid, lo = split3(x)
    return jnp.concatenate([hi, hi, mid, hi, lo, mid], axis=0)


def right_six(x):
    hi, mid, lo = split3(x)
    return jnp.concatenate([hi, mid, hi, lo, hi, mid], axis=0)


def exchange_kernel(
    gg_hbm, eg_hbm, qg_hbm, gd_hbm, ed_hbm, qd_hbm,
    full_g, full_d, left_g, right_g, left_d, coeff_d,
    gg, eg, qg, gd, ed, qd, mg_in, md_in, mg, md,
    sg_part, sg_sib, sg_half, rs_g, sg,
    sfg, sfg_sib, msg_g, z1_g, x1_g, mid_g, z2_g, x2_g, sum_g,
    sd_part, sd_sib, msg_d, z1_d, x1_d, mid_d, z2_d, x2_d, sd,
    sfd, sfd_sib, sfd_half, rs_d, own_g, own_d, co_d,
    load_sem, send_sem, recv_sem,
):
    dp, t = lax.axis_index("dp"), lax.axis_index("tensor")
    z, c = dp // 2, dp % 2
    x, y = t // 4, t % 4
    sibling = (dp + 1 - 2 * c, t)
    z_peers = [(lax.rem(z + i, Z), (2 * lax.rem(z + i, Z) + c, t)) for i in Z_ORDER]
    xy_peers = [(dp, lax.rem(x + dx, 4) * 4 + lax.rem(y + dy, 4)) for dx, dy in XY_ORDER]

    barrier = pltpu.get_barrier_semaphore()
    for device in [sibling] + [d for _, d in z_peers] + xy_peers:
        pl.semaphore_signal(barrier, inc=1, device_id=device, device_id_type=MESH)

    loads = [
        pltpu.make_async_copy(src, dst, load_sem.at[i])
        for i, (src, dst) in enumerate(
            ((qd_hbm, qd), (gd_hbm, gd), (ed_hbm, ed), (qg_hbm, qg), (gg_hbm, gg), (eg_hbm, eg))
        )
    ]
    for load in loads:
        load.start()

    def send(stage, src, dst, device):
        pltpu.make_async_remote_copy(
            src_ref=src, dst_ref=dst, send_sem=send_sem.at[stage], recv_sem=recv_sem.at[stage],
            device_id=device, device_id_type=MESH,
        ).start()

    def received(stage, ref):
        pltpu.make_async_copy(ref, ref, recv_sem.at[stage]).wait()

    def sent(stage, ref):
        pltpu.make_async_copy(ref, ref, send_sem.at[stage]).wait()

    blocks = gg.shape[0] // BLOCK
    g_half, d_half = mg_in.shape[0], md_in.shape[0]
    for load in loads[:3]:
        load.wait()
    sd_sum = None
    for b in range(blocks):
        cols = pl.ds(b * BLOCK, BLOCK)
        block = gd[:, cols].astype(F32) + ed[:, cols]
        full_d[:, cols] = block
        term = dot6(rows3(qd[:, cols]), split3(block), NT)
        sd_sum = term if sd_sum is None else sd_sum + term
    sd_part[0] = sd_sum[:, :LANES]
    sd_part[1] = sd_sum[:, LANES:]
    for load in loads[3:]:
        load.wait()
    qg3 = rows3(qg[...])
    for b in range(blocks):
        rows = pl.ds(b * BLOCK, BLOCK)
        block = gg[rows, :].astype(F32) + eg[rows, :]
        full_g[rows, :] = block
        term = dot6(qg3, split3(block), NT)
        sg_part[2 * b] = term[:, :LANES]
        sg_part[2 * b + 1] = term[:, LANES:]

    pl.semaphore_wait(barrier, 1 + len(z_peers) + len(xy_peers))

    mine, other = OWNERS * c, OWNERS * (1 - c)
    send(0, sd_part.at[1 - c], sd_sib, sibling)
    send(1, sg_part.at[pl.ds(other, OWNERS)], sg_sib, sibling)
    send(20, full_d.at[pl.ds(pl.multiple_of((1 - c) * d_half, LANES), d_half)], md_in, sibling)
    send(21, full_g.at[pl.ds(pl.multiple_of((1 - c) * g_half, LANES), g_half)], mg_in, sibling)

    def reduce_first(base, value, msg, z1, x1):
        msg[...] = value
        z1[z] = msg[0:16]
        high = msg.at[pl.ds(16, msg.shape[0] - 16)]
        x1[t] = high[...]
        for device in xy_peers:
            send(base + 1, high, x1.at[t], device)
        for _, device in z_peers:
            send(base, msg.at[pl.ds(0, 16)], z1.at[z], device)

    def reduce_second(base, z1, x1, mid, z2, x2):
        received(base, z1.at[pl.ds(0, Z - 1)])
        low = total(z1, Z)
        mid[0:16] = low
        x2[t] = low
        for device in xy_peers:
            send(base + 3, mid.at[pl.ds(0, 16)], x2.at[t], device)
        received(base + 1, x1.at[pl.ds(0, XY - 1)])
        high = total(x1, XY)
        mid[16:32] = high[0:16]
        z2[z] = high[0:16]
        for _, device in z_peers:
            send(base + 2, mid.at[pl.ds(16, 16)], z2.at[z], device)
        return high[16:]

    def reduce_third(base, z2, x2, full):
        received(base + 2, z2.at[pl.ds(0, Z - 1)])
        received(base + 3, x2.at[pl.ds(0, XY - 1)])
        full[c, 0:16] = total(x2, XY)
        full[c, 16:32] = total(z2, Z)
        send(base + 4, full.at[c], full.at[c], sibling)

    def scatter(stage, half, rs):
        for peer, device in z_peers:
            @pl.when(peer < OWNERS)
            def _():
                send(stage, half.at[peer], rs.at[z], device)

        @pl.when(z < OWNERS)
        def _():
            rs[z] = half[z]

    def gather(stage, own, dst):
        @pl.when(z < OWNERS)
        def _():
            dst[mine + z] = own[...]
            for _, device in z_peers:
                send(stage, own, dst.at[mine + z], device)

    def gathered(stage, dst):
        @pl.when(z < OWNERS)
        def _():
            received(stage, dst.at[pl.ds(0, OWNERS - 1)])

        @pl.when(z == OWNERS)
        def _():
            received(stage, dst.at[pl.ds(0, OWNERS)])

    received(0, sd_sib)
    reduce_first(2, sd_part[c] + sd_sib[...], msg_d, z1_d, x1_d)
    received(1, sg_sib)
    for i in range(OWNERS):
        sg_half[i] = sg_part[mine + i] + sg_sib[i]
    scatter(7, sg_half, rs_g)

    received(20, md_in)
    for b in range(blocks):
        cols = pl.ds(b * BLOCK, BLOCK)
        block = full_d[pl.ds(pl.multiple_of(c * d_half, LANES), d_half), cols] + md_in[:, cols]
        hi, mid, lo = split3(block)
        md[0:d_half, cols] = hi
        md[d_half : 2 * d_half, cols] = mid
        md[2 * d_half :, cols] = lo
    received(21, mg_in)
    for b in range(OWNERS):
        parts = split3(full_g[pl.ds(pl.multiple_of(c * g_half + b * LANES, LANES), LANES), :] + mg_in[pl.ds(b * LANES, LANES), :])
        for i in range(3):
            mg[i, pl.ds(b * LANES, LANES), :] = parts[i]

    reduce_second(2, z1_d, x1_d, mid_d, z2_d, x2_d)

    @pl.when(z < OWNERS)
    def _():
        received(7, rs_g.at[pl.ds(0, Z - 1)])
        own_g[...] = total(rs_g, Z)

    gather(8, own_g, sg)

    reduce_third(2, z2_d, x2_d, sd)

    hi, mid, lo = split3(sd[c])
    stacked = jnp.concatenate(
        [
            jnp.concatenate([hi, hi], axis=1),
            jnp.concatenate([mid, mid], axis=1),
            jnp.concatenate([lo, jnp.zeros_like(lo)], axis=1),
        ],
        axis=0,
    )
    for b in range(blocks):
        cols = pl.ds(b * BLOCK, BLOCK)
        a = dot(stacked, md[0 : 2 * d_half, cols], NN)
        small = dot(hi, md[2 * d_half :, cols], NN) + a[2 * RANK :]
        term = a[:RANK] + (a[RANK : 2 * RANK] + small)
        sfd[2 * b] = term[:, :LANES]
        sfd[2 * b + 1] = term[:, LANES:]
    send(9, sfd.at[pl.ds(other, OWNERS)], sfd_sib, sibling)

    gathered(8, sg)
    send(10, sg.at[pl.ds(mine, OWNERS)], sg.at[pl.ds(mine, OWNERS)], sibling)
    sfg_sum = None
    gram_sum = None
    for b in range(0, OWNERS, 2):
        n = min(2, OWNERS - b)
        rows = pl.ds(b * LANES, n * LANES)
        tile = jnp.concatenate([sg[mine + b + i] for i in range(n)], axis=1)
        term = dot6(rows3(tile), [mg[i, rows, :] for i in range(3)], NN)
        sfg_sum = term if sfg_sum is None else sfg_sum + term
        pad = jnp.zeros((LANES - RANK, n * LANES), F32)
        term = dot_high(tile, jnp.concatenate([tile, pad], axis=0), NT)
        gram_sum = term if gram_sum is None else gram_sum + term
    packed = gram_sum[0:8]
    for i in range(1, 4):
        packed = packed + pltpu.roll(gram_sum[8 * i : 8 * i + 8], RANK * i, 1)
    for i in range(2):
        sfg[i, 0:RANK] = sfg_sum[:, i * LANES : (i + 1) * LANES]
        sfg[i, RANK:] = packed
    send(12, sfg.at[1 - c], sfg_sib, sibling)

    received(9, sfd_sib)
    for i in range(OWNERS):
        sfd_half[i] = sfd[mine + i] + sfd_sib[i]
    scatter(11, sfd_half, rs_d)

    received(12, sfg_sib)
    reduce_first(13, sfg[c] + sfg_sib[...], msg_g, z1_g, x1_g)

    received(6, sd.at[1 - c])
    sketch_d = jnp.concatenate([sd[0], sd[1]], axis=1)
    pad = jnp.zeros((LANES - RANK, BLOCK), F32)
    lower_d, inv_d = eliminate(dot_high(sketch_d, jnp.concatenate([sketch_d, pad], axis=0), NT))

    @pl.when(z < OWNERS)
    def _():
        received(11, rs_d.at[pl.ds(0, Z - 1)])
        own_d[...] = dot_high(lower_d, total(rs_d, Z), NN) * (inv_d * (1.0 / 16.0))

    gather(18, own_d, co_d)
    left_d[...] = jnp.transpose(left_six(dot_high(lower_d, sketch_d, NN)))

    gram_packed = reduce_second(13, z1_g, x1_g, mid_g, z2_g, x2_g)
    lane = lax.broadcasted_iota(jnp.int32, (8, LANES), 1)
    gram_g = jnp.concatenate(
        [jnp.where(lane < RANK, gram_packed if i == 0 else pltpu.roll(gram_packed, LANES - RANK * i, 1), 0.0) for i in range(4)],
        axis=0,
    )
    lower_g, inv_g = eliminate(gram_g)
    received(10, sg.at[pl.ds(other, OWNERS)])
    for i in range(2 * OWNERS):
        left_g[pl.ds(i * LANES, LANES), :] = jnp.transpose(left_six(dot_high(lower_g, sg[i], NN)))

    gathered(18, co_d)
    send(19, co_d.at[pl.ds(mine, OWNERS)], co_d.at[pl.ds(mine, OWNERS)], sibling)

    reduce_third(13, z2_g, x2_g, sum_g)
    received(17, sum_g.at[1 - c])
    coeff = dot_high(lower_g, jnp.concatenate([sum_g[0], sum_g[1]], axis=1), NN) * (inv_g * (1.0 / 16.0))
    right_g[...] = right_six(coeff)
    received(19, co_d.at[pl.ds(other, OWNERS)])
    coeff_d[...] = co_d[...]

    sent(0, sd_sib)
    sent(1, sg_sib)
    sent(20, md_in)
    sent(21, mg_in)
    sent(9, sfd_sib)
    sent(12, sfg_sib)
    sent(10, sg_sib)
    sent(19, sg_sib)
    for base, z1, x1, z2, x2, full in (
        (2, z1_d, x1_d, z2_d, x2_d, sd),
        (13, z1_g, x1_g, z2_g, x2_g, sum_g),
    ):
        sent(base, z1.at[pl.ds(0, Z - 1)])
        sent(base + 1, x1.at[pl.ds(0, XY - 1)])
        sent(base + 2, z2.at[pl.ds(0, Z - 1)])
        sent(base + 3, x2.at[pl.ds(0, XY - 1)])
        sent(base + 4, full.at[0])
    for scatter_stage, gather_stage, rs in ((7, 8, rs_g), (11, 18, rs_d)):
        @pl.when(z < OWNERS)
        def _():
            sent(scatter_stage, rs.at[pl.ds(0, OWNERS - 1)])
            sent(gather_stage, rs.at[pl.ds(0, Z - 1)])

        @pl.when(z == OWNERS)
        def _():
            sent(scatter_stage, rs.at[pl.ds(0, OWNERS)])


def finish_kernel(full_g, full_d, left_g, right_g, left_d, coeff_d, ug_hbm, ng_hbm, ud_hbm, nd_hbm, ug, ng, ud, nd, sem):
    copies = []

    def store(src, dst):
        copies.append(pltpu.make_async_copy(src, dst, sem.at[len(copies)]))
        copies[-1].start()

    for b in range(full_g.shape[0] // BLOCK):
        part = (pl.ds(b * BLOCK, BLOCK), slice(None))
        update = dot(left_g[part], right_g[...], NN)
        ug[part] = update
        ng[part] = full_g[part] - update
        store(ug.at[part], ug_hbm.at[part])
        store(ng.at[part], ng_hbm.at[part])
        part = (slice(None), pl.ds(b * BLOCK, BLOCK))
        right = right_six(jnp.concatenate([coeff_d[2 * b], coeff_d[2 * b + 1]], axis=1))
        update = dot(left_d[...], right, NN)
        ud[part] = update
        nd[part] = full_d[part] - update
        store(ud.at[part], ud_hbm.at[part])
        store(nd.at[part], nd_hbm.at[part])
    for copy in copies:
        copy.wait()


def local(grad_gate, error_gate, query_gate, grad_down, error_down, query_down):
    gg, eg, gd, ed = grad_gate[0], error_gate[0], grad_down[0], error_down[0]
    ff, rows = gg.shape
    tiles = ff // LANES
    vmem = pltpu.VMEM
    tile = (RANK, LANES)

    def stack(n, r=RANK):
        return vmem((n, r, LANES), F32)

    def reduce_buffers(extra):
        return [vmem((RANK + extra, LANES), F32), stack(Z, 16), stack(XY, 16 + extra), vmem(tile, F32), stack(Z, 16), stack(XY, 16), stack(2)]

    scratch = (
        [vmem((ff, rows), BF16), vmem((ff, rows), F32), vmem((RANK, rows), F32)]
        + [vmem((rows, ff), BF16), vmem((rows, ff), F32), vmem((RANK, ff), F32)]
        + [vmem((ff // 2, rows), F32), vmem((rows // 2, ff), F32), vmem((3, ff // 2, rows), BF16), vmem((3 * rows // 2, ff), BF16)]
        + [stack(tiles), stack(OWNERS), stack(OWNERS), stack(Z), stack(tiles)]
        + [stack(2, RANK + 8), vmem((RANK + 8, LANES), F32)] + reduce_buffers(8)
        + [stack(2), vmem(tile, F32)] + reduce_buffers(0)
        + [stack(tiles), stack(OWNERS), stack(OWNERS), stack(Z), vmem(tile, F32), vmem(tile, F32), stack(tiles)]
        + [pltpu.SemaphoreType.DMA((6,)), pltpu.SemaphoreType.DMA((22,)), pltpu.SemaphoreType.DMA((22,))]
    )
    whole = pl.BlockSpec(memory_space=pltpu.VMEM)
    gate_shape, down_shape = (ff, rows), (rows, ff)
    shapes = [
        (gate_shape, F32), (down_shape, F32), ((ff, 6 * RANK), BF16), ((6 * RANK, rows), BF16),
        ((rows, 6 * RANK), BF16), ((tiles, RANK, LANES), F32),
    ]
    inputs = [pltpu.with_memory_space_constraint(a, pltpu.HBM) for a in (gg, eg, query_gate, gd, ed, query_down)]
    middle = pl.pallas_call(
        exchange_kernel,
        out_shape=[pltpu.VMEM(shape, dtype) for shape, dtype in shapes],
        in_specs=[pl.BlockSpec(memory_space=pltpu.HBM)] * 6,
        out_specs=[whole] * len(shapes),
        scratch_shapes=scratch,
        compiler_params=pltpu.CompilerParams(collective_id=0, has_side_effects=True, vmem_limit_bytes=32 * 2**20),
    )(*inputs)

    outs = [gate_shape, gate_shape, down_shape, down_shape]
    ug, ng, ud, nd = pl.pallas_call(
        finish_kernel,
        out_shape=[jax.ShapeDtypeStruct(shape, F32) for shape in outs],
        in_specs=[whole] * len(shapes),
        out_specs=[pl.BlockSpec(memory_space=pl.ANY)] * 4,
        scratch_shapes=[vmem(shape, F32) for shape in outs] + [pltpu.SemaphoreType.DMA((4 * (ff // BLOCK),))],
        compiler_params=pltpu.CompilerParams(vmem_limit_bytes=32 * 2**20),
    )(*middle)
    return ug, ng[None], ud, nd[None]


def solution(mesh):
    in_specs = (
        P("dp", "tensor", None),
        P("dp", "tensor", None),
        P(),
        P("dp", None, "tensor"),
        P("dp", None, "tensor"),
        P(None, "tensor"),
    )
    out_specs = (
        P("tensor", None),
        P("dp", "tensor", None),
        P(None, "tensor"),
        P("dp", None, "tensor"),
    )
    return jax.shard_map(local, mesh=mesh, in_specs=in_specs, out_specs=out_specs, check_vma=False)
```

```python
import functools

import jax
import jax.numpy as jnp
from jax import lax
from jax.experimental import pallas as pl
from jax.experimental.pallas import tpu as pltpu
from jax.sharding import PartitionSpec as P

MESH = pl.DeviceIdType.MESH
F32, BF16 = jnp.float32, jnp.bfloat16
NN = (((1,), (0,)), ((), ()))
NT = (((1,), (1,)), ((), ()))
TN = (((0,), (0,)), ((), ()))
LANES = 128
BLOCK = 256
RANK = 32
Z, XY = 8, 16
HALF = 7
CHUNK = 4
SPREAD = 16
Z_ORDER = (4, 3, 5, 2, 6, 1, 7)
XY_ORDER = sorted(
    ((dx, dy) for dx in range(4) for dy in range(4) if dx or dy),
    key=lambda o: -(min(o[0], 4 - o[0]) + min(o[1], 4 - o[1])),
)


def split3(x):
    hi = x.astype(BF16)
    rest = x - hi.astype(F32)
    mid = rest.astype(BF16)
    return hi, mid, (rest - mid.astype(F32)).astype(BF16)


def rows3(x):
    return jnp.concatenate(split3(x), axis=0)


def dot(a, b, dims):
    return lax.dot_general(a, b, dims, preferred_element_type=F32)


def dot6(left3, right, dims):
    hi, mid, lo = right
    a = dot(left3, hi, dims)
    b = dot(left3[: 2 * RANK], mid, dims)
    c = dot(left3[:RANK], lo, dims)
    small = a[2 * RANK :] + b[RANK:] + c
    return a[:RANK] + ((a[RANK : 2 * RANK] + b[:RANK]) + small)


def tile_of(ref, half, i):
    return jnp.concatenate([ref[half, k, CHUNK * i : CHUNK * (i + 1)] for k in range(Z)], axis=0)


def put_tile(ref, j, tile):
    i = CHUNK * (j % HALF)
    for k in range(Z):
        ref[j // HALF, k, i : i + CHUNK] = tile[k * CHUNK : (k + 1) * CHUNK]


def total(ref, n):
    out = ref[0]
    for i in range(1, n):
        out = out + ref[i]
    return out


def eliminate(gram):
    rows = lax.broadcasted_iota(jnp.int32, (RANK, LANES), 0)
    lanes = lax.broadcasted_iota(jnp.int32, (RANK, LANES), 1)
    a = gram + (lanes == rows + RANK).astype(F32)
    for first in range(0, RANK, SPREAD):
        columns = [jnp.broadcast_to(a[:, k : k + 1], (RANK, LANES)) for k in range(first, first + SPREAD)]
        for i, column in enumerate(columns):
            k = first + i
            factor = jnp.where(rows > k, column, 0.0) * (1.0 / column[k : k + 1])
            for later in range(i + 1, SPREAD):
                columns[later] = columns[later] - factor * columns[later][k : k + 1]
            a = a - factor * a[k : k + 1]
    pivots = jnp.sum(jnp.where(lanes == rows, a, 0.0), axis=1, keepdims=True)
    return a[:, RANK : 2 * RANK], jnp.transpose(a)[RANK : 2 * RANK], 1.0 / pivots


def left_six(x):
    hi, mid, lo = split3(x)
    return jnp.concatenate([hi, hi, mid, hi, lo, mid], axis=0)


def left_lanes(x):
    hi, mid, lo = split3(x)
    return jnp.concatenate([hi, hi, mid, hi, lo, mid], axis=1)


def right_six(x):
    hi, mid, lo = split3(x)
    return jnp.concatenate([hi, mid, hi, lo, hi, mid], axis=0)


def exchange_kernel(
    gg_hbm, eg_hbm, qg_hbm, gd_hbm, ed_hbm, qd_hbm,
    full_g, full_d, left_g, right_g, left_d, coeff_d,
    gg, eg, qg, gd, ed, qd, mg_in, md_in, mg, md,
    sg_part, sg_sib, sg_half, rs_g, sg,
    sfg, sfg_sib, gram_own, gram_sib, msg_g, z1_g, x1_g, mid_g, z2_g, x2_g, sum_g,
    sd_part, sd_sib, msg_d, z1_d, x1_d, mid_d, z2_d, x2_d, sd,
    sfd, sfd_sib, sfd_half, rs_d, own_g, own_d, co_d,
    load_sem, send_sem, recv_sem,
):
    dp, t = lax.axis_index("dp"), lax.axis_index("tensor")
    z, c = dp // 2, dp % 2
    x, y = t // 4, t % 4
    sibling = (dp + 1 - 2 * c, t)
    z_peers = [(lax.rem(z + i, Z), (2 * lax.rem(z + i, Z) + c, t)) for i in Z_ORDER]
    xy_peers = [(dp, lax.rem(x + dx, 4) * 4 + lax.rem(y + dy, 4)) for dx, dy in XY_ORDER]

    barrier = pltpu.get_barrier_semaphore()
    for device in [sibling] + [d for _, d in z_peers] + xy_peers:
        pl.semaphore_signal(barrier, inc=1, device_id=device, device_id_type=MESH)

    loads = [
        pltpu.make_async_copy(src, dst, load_sem.at[i])
        for i, (src, dst) in enumerate(
            ((qd_hbm, qd), (gd_hbm, gd), (ed_hbm, ed), (qg_hbm, qg), (gg_hbm, gg), (eg_hbm, eg))
        )
    ]
    for load in loads:
        load.start()

    def send(stage, src, dst, device):
        pltpu.make_async_remote_copy(
            src_ref=src, dst_ref=dst, send_sem=send_sem.at[stage], recv_sem=recv_sem.at[stage],
            device_id=device, device_id_type=MESH,
        ).start()

    def received(stage, ref):
        pltpu.make_async_copy(ref, ref, recv_sem.at[stage]).wait()

    def sent(stage, ref):
        pltpu.make_async_copy(ref, ref, send_sem.at[stage]).wait()

    blocks = gg.shape[0] // BLOCK
    g_half, d_half = mg_in.shape[0], md_in.shape[0]
    for load in loads[:3]:
        load.wait()
    sd_sum = None
    for b in range(blocks):
        cols = pl.ds(b * BLOCK, BLOCK)
        block = gd[:, cols].astype(F32) + ed[:, cols]
        full_d[:, cols] = block
        term = dot6(rows3(qd[:, cols]), split3(block), NT)
        sd_sum = term if sd_sum is None else sd_sum + term
    sd_part[0] = sd_sum[:, :LANES]
    sd_part[1] = sd_sum[:, LANES:]
    for load in loads[3:]:
        load.wait()
    qg3 = rows3(qg[...])
    for b in range(blocks):
        rows = pl.ds(b * BLOCK, BLOCK)
        block = gg[rows, :].astype(F32) + eg[rows, :]
        full_g[rows, :] = block
        term = dot6(qg3, split3(block), NT)
        put_tile(sg_part, 2 * b, term[:, :LANES])
        put_tile(sg_part, 2 * b + 1, term[:, LANES:])

    pl.semaphore_wait(barrier, 1 + len(z_peers) + len(xy_peers))

    send(1, sg_part.at[1 - c], sg_sib, sibling)
    send(0, sd_part.at[1 - c], sd_sib, sibling)

    def reduce_first(base, value, msg, z1, x1):
        msg[...] = value
        z1[z] = msg[0:16]
        high = msg.at[pl.ds(16, msg.shape[0] - 16)]
        x1[t] = high[...]
        for device in xy_peers:
            send(base + 1, high, x1.at[t], device)
        for _, device in z_peers:
            send(base, msg.at[pl.ds(0, 16)], z1.at[z], device)

    def reduce_second(base, z1, x1, mid, z2, x2):
        received(base, z1.at[pl.ds(0, Z - 1)])
        low = total(z1, Z)
        mid[0:16] = low
        x2[t] = low
        for device in xy_peers:
            send(base + 3, mid.at[pl.ds(0, 16)], x2.at[t], device)
        received(base + 1, x1.at[pl.ds(0, XY - 1)])
        high = total(x1, XY)
        mid[16:32] = high[0:16]
        z2[z] = high[0:16]
        for _, device in z_peers:
            send(base + 2, mid.at[pl.ds(16, 16)], z2.at[z], device)
        return high[16:]

    def reduce_third(base, z2, x2, full):
        received(base + 2, z2.at[pl.ds(0, Z - 1)])
        received(base + 3, x2.at[pl.ds(0, XY - 1)])
        full[c, 0:16] = total(x2, XY)
        full[c, 16:32] = total(z2, Z)
        send(base + 4, full.at[c], full.at[c], sibling)

    def scatter(stage, part, sib, half, rs):
        for k in range(Z):
            half[k] = part[c, k] + sib[k]
        for peer, device in z_peers:
            send(stage, half.at[peer], rs.at[z], device)
        rs[z] = half[z]

    def gather(stage, rs_stage, rs, own, dst):
        received(rs_stage, rs.at[pl.ds(0, Z - 1)])
        own[...] = total(rs, Z)
        for _, device in z_peers:
            send(stage, own, dst.at[c, z], device)
        dst[c, z] = own[...]

    def gathered(stage, dst):
        received(stage, dst.at[c, pl.ds(0, Z - 1)])

    received(1, sg_sib)
    scatter(7, sg_part, sg_sib, sg_half, rs_g)
    received(0, sd_sib)
    reduce_first(2, sd_part[c] + sd_sib[...], msg_d, z1_d, x1_d)
    send(20, full_d.at[pl.ds(pl.multiple_of((1 - c) * d_half, LANES), d_half)], md_in, sibling)
    send(21, full_g.at[pl.ds(pl.multiple_of((1 - c) * g_half, LANES), g_half)], mg_in, sibling)

    received(20, md_in)
    for b in range(blocks):
        cols = pl.ds(b * BLOCK, BLOCK)
        block = full_d[pl.ds(pl.multiple_of(c * d_half, LANES), d_half), cols] + md_in[:, cols]
        hi, mid, lo = split3(block)
        md[0:d_half, cols] = hi
        md[d_half : 2 * d_half, cols] = mid
        md[2 * d_half :, cols] = lo
    received(21, mg_in)
    for b in range(HALF):
        parts = split3(full_g[pl.ds(pl.multiple_of(c * g_half + b * LANES, LANES), LANES), :] + mg_in[pl.ds(b * LANES, LANES), :])
        for i in range(3):
            mg[i, pl.ds(b * LANES, LANES), :] = parts[i]

    gather(8, 7, rs_g, own_g, sg)

    reduce_second(2, z1_d, x1_d, mid_d, z2_d, x2_d)

    gathered(8, sg)
    tiles = [jnp.concatenate([tile_of(sg, c, i) for i in range(b, min(b + 2, HALF))], axis=1) for b in range(0, HALF, 2)]
    sfg_sum = None
    for b, tile in enumerate(tiles):
        rows = pl.ds(b * BLOCK, tile.shape[1])
        term = dot6(rows3(tile), [mg[i, rows, :] for i in range(3)], NN)
        sfg_sum = term if sfg_sum is None else sfg_sum + term
    for i in range(2):
        sfg[i] = sfg_sum[:, i * LANES : (i + 1) * LANES]
    send(12, sfg.at[1 - c], sfg_sib, sibling)
    gram_sum = None
    for tile in tiles:
        pad = jnp.zeros((LANES - RANK, tile.shape[1]), F32)
        term = dot6(rows3(tile), split3(jnp.concatenate([tile, pad], axis=0)), NT)
        gram_sum = term if gram_sum is None else gram_sum + term
    packed = gram_sum[0:8]
    for i in range(1, 4):
        packed = packed + pltpu.roll(gram_sum[8 * i : 8 * i + 8], RANK * i, 1)
    gram_own[...] = packed
    send(22, gram_own, gram_sib, sibling)

    received(12, sfg_sib)
    received(22, gram_sib)
    reduce_first(13, jnp.concatenate([sfg[c] + sfg_sib[...], gram_own[...] + gram_sib[...]], axis=0), msg_g, z1_g, x1_g)

    reduce_third(2, z2_d, x2_d, sd)

    hi, mid, lo = split3(sd[c])
    stacked = jnp.concatenate(
        [
            jnp.concatenate([hi, hi], axis=1),
            jnp.concatenate([mid, mid], axis=1),
            jnp.concatenate([lo, jnp.zeros_like(lo)], axis=1),
        ],
        axis=0,
    )
    for b in range(blocks):
        cols = pl.ds(b * BLOCK, BLOCK)
        a = dot(stacked, md[0 : 2 * d_half, cols], NN)
        small = dot(hi, md[2 * d_half :, cols], NN) + a[2 * RANK :]
        term = a[:RANK] + (a[RANK : 2 * RANK] + small)
        put_tile(sfd, 2 * b, term[:, :LANES])
        put_tile(sfd, 2 * b + 1, term[:, LANES:])
    send(9, sfd.at[1 - c], sfd_sib, sibling)

    received(9, sfd_sib)
    scatter(11, sfd, sfd_sib, sfd_half, rs_d)
    send(10, sg.at[c], sg.at[c], sibling)

    received(6, sd.at[1 - c])
    sketch_d = jnp.concatenate([sd[0], sd[1]], axis=1)
    pad = jnp.zeros((LANES - RANK, BLOCK), F32)
    lower_d, upper_d, inv_d = eliminate(dot6(rows3(sketch_d), split3(jnp.concatenate([sketch_d, pad], axis=0)), NT))
    solved = dot(left_lanes(lower_d), right_six(sketch_d), NN) * (inv_d * (1.0 / 16.0))
    left_d[...] = jnp.transpose(left_six(dot(left_lanes(upper_d), right_six(solved), NN)))

    gram_packed = reduce_second(13, z1_g, x1_g, mid_g, z2_g, x2_g)

    gather(18, 11, rs_d, own_d, co_d)

    lane = lax.broadcasted_iota(jnp.int32, (8, LANES), 1)
    gram_g = jnp.concatenate(
        [jnp.where(lane < RANK, gram_packed if i == 0 else pltpu.roll(gram_packed, LANES - RANK * i, 1), 0.0) for i in range(4)],
        axis=0,
    )
    lower_g, _, inv_g = eliminate(gram_g)
    lower_g = left_lanes(lower_g)
    received(10, sg.at[1 - c])
    for i in range(HALF):
        tile = jnp.concatenate([tile_of(sg, j // HALF, j % HALF) for j in (2 * i, 2 * i + 1)], axis=1)
        left_g[pl.ds(i * BLOCK, BLOCK), :] = jnp.transpose(left_six(dot(lower_g, right_six(tile), NN)))

    reduce_third(13, z2_g, x2_g, sum_g)
    gathered(18, co_d)
    send(19, co_d.at[c], co_d.at[c], sibling)
    received(17, sum_g.at[1 - c])
    coeff = dot(lower_g, right_six(jnp.concatenate([sum_g[0], sum_g[1]], axis=1)), NN) * (inv_g * (1.0 / 16.0))
    right_g[...] = right_six(coeff)
    received(19, co_d.at[1 - c])
    coeff_d[...] = co_d[...]

    sent(0, sd_sib)
    sent(1, sg_sib)
    sent(20, md_in)
    sent(21, mg_in)
    sent(9, sfd_sib)
    sent(12, sfg_sib)
    sent(22, gram_sib)
    sent(10, sg_sib)
    sent(19, sg_sib)
    for base, z1, x1, z2, x2, full in (
        (2, z1_d, x1_d, z2_d, x2_d, sd),
        (13, z1_g, x1_g, z2_g, x2_g, sum_g),
    ):
        sent(base, z1.at[pl.ds(0, Z - 1)])
        sent(base + 1, x1.at[pl.ds(0, XY - 1)])
        sent(base + 2, z2.at[pl.ds(0, Z - 1)])
        sent(base + 3, x2.at[pl.ds(0, XY - 1)])
        sent(base + 4, full.at[0])
    for stage, rs in ((7, rs_g), (8, rs_g), (11, rs_d), (18, rs_d)):
        sent(stage, rs.at[pl.ds(0, Z - 1)])


def finish_kernel(full_g, full_d, left_g, right_g, left_d, coeff_d, ug_hbm, ng_hbm, ud_hbm, nd_hbm, ug, ng, ud, nd, sem):
    copies = []

    def store(src, dst):
        copies.append(pltpu.make_async_copy(src, dst, sem.at[len(copies)]))
        copies[-1].start()

    for b in range(full_g.shape[0] // BLOCK):
        part = (pl.ds(b * BLOCK, BLOCK), slice(None))
        update = dot(left_g[part], right_g[...], NN)
        ug[part] = update
        ng[part] = full_g[part] - update
        store(ug.at[part], ug_hbm.at[part])
        store(ng.at[part], ng_hbm.at[part])
        part = (slice(None), pl.ds(b * BLOCK, BLOCK))
        right = right_six(jnp.concatenate([tile_of(coeff_d, j // HALF, j % HALF) for j in (2 * b, 2 * b + 1)], axis=1))
        update = dot(left_d[...], right, NN)
        ud[part] = update
        nd[part] = full_d[part] - update
        store(ud.at[part], ud_hbm.at[part])
        store(nd.at[part], nd_hbm.at[part])
    for copy in copies:
        copy.wait()


def local(grad_gate, error_gate, query_gate, grad_down, error_down, query_down):
    gg, eg, gd, ed = grad_gate[0], error_gate[0], grad_down[0], error_down[0]
    ff, rows = gg.shape
    vmem = pltpu.VMEM
    tile = (RANK, LANES)
    half = (Z, HALF * CHUNK, LANES)
    chunk, both = vmem(half[1:], F32), vmem((2, *half), F32)

    def stack(n, r=RANK):
        return vmem((n, r, LANES), F32)

    def reduce_buffers(extra):
        return [vmem((RANK + extra, LANES), F32), stack(Z, 16), stack(XY, 16 + extra), vmem(tile, F32), stack(Z, 16), stack(XY, 16), stack(2)]

    scratch = (
        [vmem((ff, rows), BF16), vmem((ff, rows), F32), vmem((RANK, rows), F32)]
        + [vmem((rows, ff), BF16), vmem((rows, ff), F32), vmem((RANK, ff), F32)]
        + [vmem((ff // 2, rows), F32), vmem((rows // 2, ff), F32), vmem((3, ff // 2, rows), BF16), vmem((3 * rows // 2, ff), BF16)]
        + [both, vmem(half, F32), vmem(half, F32), vmem(half, F32), both]
        + [stack(2), vmem(tile, F32), vmem((8, LANES), F32), vmem((8, LANES), F32)] + reduce_buffers(8)
        + [stack(2), vmem(tile, F32)] + reduce_buffers(0)
        + [both, vmem(half, F32), vmem(half, F32), vmem(half, F32), chunk, chunk, both]
        + [pltpu.SemaphoreType.DMA((6,)), pltpu.SemaphoreType.DMA((23,)), pltpu.SemaphoreType.DMA((23,))]
    )
    whole = pl.BlockSpec(memory_space=pltpu.VMEM)
    gate_shape, down_shape = (ff, rows), (rows, ff)
    shapes = [
        (gate_shape, F32), (down_shape, F32), ((ff, 6 * RANK), BF16), ((6 * RANK, rows), BF16),
        ((rows, 6 * RANK), BF16), ((2, *half), F32),
    ]
    inputs = [pltpu.with_memory_space_constraint(a, pltpu.HBM) for a in (gg, eg, query_gate, gd, ed, query_down)]
    middle = pl.pallas_call(
        exchange_kernel,
        out_shape=[pltpu.VMEM(shape, dtype) for shape, dtype in shapes],
        in_specs=[pl.BlockSpec(memory_space=pltpu.HBM)] * 6,
        out_specs=[whole] * len(shapes),
        scratch_shapes=scratch,
        compiler_params=pltpu.CompilerParams(collective_id=0, has_side_effects=True, vmem_limit_bytes=32 * 2**20),
    )(*inputs)

    outs = [gate_shape, gate_shape, down_shape, down_shape]
    ug, ng, ud, nd = pl.pallas_call(
        finish_kernel,
        out_shape=[jax.ShapeDtypeStruct(shape, F32) for shape in outs],
        in_specs=[whole] * len(shapes),
        out_specs=[pl.BlockSpec(memory_space=pl.ANY)] * 4,
        scratch_shapes=[vmem(shape, F32) for shape in outs] + [pltpu.SemaphoreType.DMA((4 * (ff // BLOCK),))],
        compiler_params=pltpu.CompilerParams(vmem_limit_bytes=32 * 2**20),
    )(*middle)
    return ug, ng[None], ud, nd[None]


def solution(mesh):
    in_specs = (
        P("dp", "tensor", None),
        P("dp", "tensor", None),
        P(),
        P("dp", None, "tensor"),
        P("dp", None, "tensor"),
        P(None, "tensor"),
    )
    out_specs = (
        P("tensor", None),
        P("dp", "tensor", None),
        P(None, "tensor"),
        P("dp", None, "tensor"),
    )
    return jax.shard_map(local, mesh=mesh, in_specs=in_specs, out_specs=out_specs, check_vma=False)
```

```python
import functools

import jax
import jax.numpy as jnp
from jax import lax
from jax.experimental import pallas as pl
from jax.experimental.pallas import tpu as pltpu
from jax.sharding import PartitionSpec as P

MESH = pl.DeviceIdType.MESH
F32, BF16 = jnp.float32, jnp.bfloat16
NN = (((1,), (0,)), ((), ()))
NT = (((1,), (1,)), ((), ()))
TN = (((0,), (0,)), ((), ()))
LANES = 128
BLOCK = 256
RANK = 32
Z, XY = 8, 16
HALF = 7
CHUNK = 4
SPREAD = 16
Z_ORDER = (4, 3, 5, 2, 6, 1, 7)
XY_ORDER = sorted(
    ((dx, dy) for dx in range(4) for dy in range(4) if dx or dy),
    key=lambda o: -(min(o[0], 4 - o[0]) + min(o[1], 4 - o[1])),
)


def split3(x):
    hi = x.astype(BF16)
    rest = x - hi.astype(F32)
    mid = rest.astype(BF16)
    return hi, mid, (rest - mid.astype(F32)).astype(BF16)


def rows3(x):
    return jnp.concatenate(split3(x), axis=0)


def dot(a, b, dims):
    return lax.dot_general(a, b, dims, preferred_element_type=F32)


def dot6(left3, right, dims):
    hi, mid, lo = right
    a = dot(left3, hi, dims)
    b = dot(left3[: 2 * RANK], mid, dims)
    c = dot(left3[:RANK], lo, dims)
    small = a[2 * RANK :] + b[RANK:] + c
    return a[:RANK] + ((a[RANK : 2 * RANK] + b[:RANK]) + small)


def tile_of(ref, half, i):
    return jnp.concatenate([ref[half, k, CHUNK * i : CHUNK * (i + 1)] for k in range(Z)], axis=0)


def put_tile(ref, half, i, tile):
    for k in range(Z):
        ref[half, k, CHUNK * i : CHUNK * (i + 1)] = tile[k * CHUNK : (k + 1) * CHUNK]


def total(ref, n):
    out = ref[0]
    for i in range(1, n):
        out = out + ref[i]
    return out


def eliminate(gram):
    rows = lax.broadcasted_iota(jnp.int32, (RANK, LANES), 0)
    lanes = lax.broadcasted_iota(jnp.int32, (RANK, LANES), 1)
    a = gram + (lanes == rows + RANK).astype(F32)
    for first in range(0, RANK, SPREAD):
        columns = [jnp.broadcast_to(a[:, k : k + 1], (RANK, LANES)) for k in range(first, first + SPREAD)]
        for i, column in enumerate(columns):
            k = first + i
            factor = jnp.where(rows > k, column, 0.0) * (1.0 / column[k : k + 1])
            for later in range(i + 1, SPREAD):
                columns[later] = columns[later] - factor * columns[later][k : k + 1]
            a = a - factor * a[k : k + 1]
    pivots = jnp.sum(jnp.where(lanes == rows, a, 0.0), axis=1, keepdims=True)
    return a[:, RANK : 2 * RANK], jnp.transpose(a)[RANK : 2 * RANK], 1.0 / pivots


def left_six(x):
    hi, mid, lo = split3(x)
    return jnp.concatenate([hi, hi, mid, hi, lo, mid], axis=0)


def left_lanes(x):
    hi, mid, lo = split3(x)
    return jnp.concatenate([hi, hi, mid, hi, lo, mid], axis=1)


def right_six(x):
    hi, mid, lo = split3(x)
    return jnp.concatenate([hi, mid, hi, lo, hi, mid], axis=0)


def exchange_kernel(
    gg_hbm, eg_hbm, qg_hbm, gd_hbm, ed_hbm, qd_hbm,
    full_g, full_d, left_g, right_g, left_d, coeff_d,
    gg, eg, qg, gd, ed, qd, mg_in, md_in, mg, md,
    sg_part, sg_sib, sg_half, rs_g, sg,
    sfg, sfg_sib, gram_own, gram_sib, gram_pair, gram_all, msg_g, z1_g, x1_g, mid_g, z2_g, x2_g, sum_g,
    sd_part, sd_sib, msg_d, z1_d, x1_d, mid_d, z2_d, x2_d, sd,
    sfd, sfd_sib, sfd_half, rs_d, own_g, own_d, co_d,
    load_sem, send_sem, recv_sem,
):
    dp, t = lax.axis_index("dp"), lax.axis_index("tensor")
    z, c = dp // 2, dp % 2
    x, y = t // 4, t % 4
    sibling = (dp + 1 - 2 * c, t)
    z_peers = [(lax.rem(z + i, Z), (2 * lax.rem(z + i, Z) + c, t)) for i in Z_ORDER]
    xy_peers = [(dp, lax.rem(x + dx, 4) * 4 + lax.rem(y + dy, 4)) for dx, dy in XY_ORDER]

    barrier = pltpu.get_barrier_semaphore()
    for device in [sibling] + [d for _, d in z_peers] + xy_peers:
        pl.semaphore_signal(barrier, inc=1, device_id=device, device_id_type=MESH)

    loads = [
        pltpu.make_async_copy(src, dst, load_sem.at[i])
        for i, (src, dst) in enumerate(
            ((qd_hbm, qd), (gd_hbm, gd), (ed_hbm, ed), (qg_hbm, qg), (gg_hbm, gg), (eg_hbm, eg))
        )
    ]
    for load in loads:
        load.start()

    def send(stage, src, dst, device):
        pltpu.make_async_remote_copy(
            src_ref=src, dst_ref=dst, send_sem=send_sem.at[stage], recv_sem=recv_sem.at[stage],
            device_id=device, device_id_type=MESH,
        ).start()

    def received(stage, ref):
        pltpu.make_async_copy(ref, ref, recv_sem.at[stage]).wait()

    def sent(stage, ref):
        pltpu.make_async_copy(ref, ref, send_sem.at[stage]).wait()

    blocks = gg.shape[0] // BLOCK
    g_half, d_half = mg_in.shape[0], md_in.shape[0]
    for load in loads[:3]:
        load.wait()
    sd_sum = None
    for b in range(blocks):
        cols = pl.ds(b * BLOCK, BLOCK)
        block = gd[:, cols].astype(F32) + ed[:, cols]
        full_d[:, cols] = block
        term = dot6(rows3(qd[:, cols]), split3(block), NT)
        sd_sum = term if sd_sum is None else sd_sum + term
    sd_part[0] = sd_sum[:, :LANES]
    sd_part[1] = sd_sum[:, LANES:]
    for load in loads[3:]:
        load.wait()
    qg3 = rows3(qg[...])
    for b in range(blocks):
        rows = pl.ds(b * BLOCK, BLOCK)
        block = gg[rows, :].astype(F32) + eg[rows, :]
        full_g[rows, :] = block
        term = dot6(qg3, split3(block), NT)
        for j, tile in ((2 * b, term[:, :LANES]), (2 * b + 1, term[:, LANES:])):
            put_tile(sg_part, j // HALF, j % HALF, tile)

    pl.semaphore_wait(barrier, 1 + len(z_peers) + len(xy_peers))

    send(1, sg_part.at[1 - c], sg_sib, sibling)
    send(0, sd_part.at[1 - c], sd_sib, sibling)

    def reduce_first(base, value, msg, z1, x1):
        msg[...] = value
        z1[z] = msg[0:16]
        high = msg.at[pl.ds(16, msg.shape[0] - 16)]
        x1[t] = high[...]
        for device in xy_peers:
            send(base + 1, high, x1.at[t], device)
        for _, device in z_peers:
            send(base, msg.at[pl.ds(0, 16)], z1.at[z], device)

    def reduce_second(base, z1, x1, mid, z2, x2):
        received(base, z1.at[pl.ds(0, Z - 1)])
        low = total(z1, Z)
        mid[0:16] = low
        x2[t] = low
        for device in xy_peers:
            send(base + 3, mid.at[pl.ds(0, 16)], x2.at[t], device)
        received(base + 1, x1.at[pl.ds(0, XY - 1)])
        high = total(x1, XY)
        mid[16:32] = high
        z2[z] = high
        for _, device in z_peers:
            send(base + 2, mid.at[pl.ds(16, 16)], z2.at[z], device)

    def reduce_third(base, z2, x2, full):
        received(base + 2, z2.at[pl.ds(0, Z - 1)])
        received(base + 3, x2.at[pl.ds(0, XY - 1)])
        full[c, 0:16] = total(x2, XY)
        full[c, 16:32] = total(z2, Z)
        send(base + 4, full.at[c], full.at[c], sibling)

    def scatter(stage, part, sib, half, rs):
        for k in range(Z):
            half[k] = part[c, k] + sib[k]
        for peer, device in z_peers:
            send(stage, half.at[peer], rs.at[z], device)
        rs[z] = half[z]

    def gather(stage, rs_stage, rs, own, dst):
        received(rs_stage, rs.at[pl.ds(0, Z - 1)])
        own[...] = total(rs, Z)
        for _, device in z_peers:
            send(stage, own, dst.at[c, z], device)
        dst[c, z] = own[...]

    def gathered(stage, dst):
        received(stage, dst.at[c, pl.ds(0, Z - 1)])

    received(1, sg_sib)
    scatter(7, sg_part, sg_sib, sg_half, rs_g)
    received(0, sd_sib)
    reduce_first(2, sd_part[c] + sd_sib[...], msg_d, z1_d, x1_d)
    send(20, full_d.at[pl.ds(pl.multiple_of((1 - c) * d_half, LANES), d_half)], md_in, sibling)
    send(21, full_g.at[pl.ds(pl.multiple_of((1 - c) * g_half, LANES), g_half)], mg_in, sibling)

    received(20, md_in)
    for b in range(blocks):
        cols = pl.ds(b * BLOCK, BLOCK)
        block = full_d[pl.ds(pl.multiple_of(c * d_half, LANES), d_half), cols] + md_in[:, cols]
        hi, mid, lo = split3(block)
        md[0:d_half, cols] = hi
        md[d_half : 2 * d_half, cols] = mid
        md[2 * d_half :, cols] = lo
    received(21, mg_in)
    for b in range(HALF):
        parts = split3(full_g[pl.ds(pl.multiple_of(c * g_half + b * LANES, LANES), LANES), :] + mg_in[pl.ds(b * LANES, LANES), :])
        for i in range(3):
            mg[i, pl.ds(b * LANES, LANES), :] = parts[i]

    gather(8, 7, rs_g, own_g, sg)

    reduce_second(2, z1_d, x1_d, mid_d, z2_d, x2_d)

    gathered(8, sg)
    tiles = [jnp.concatenate([tile_of(sg, c, i) for i in range(b, min(b + 2, HALF))], axis=1) for b in range(0, HALF, 2)]
    sfg_sum = None
    for b, tile in enumerate(tiles):
        rows = pl.ds(b * BLOCK, tile.shape[1])
        term = dot6(rows3(tile), [mg[i, rows, :] for i in range(3)], NN)
        sfg_sum = term if sfg_sum is None else sfg_sum + term
    for i in range(2):
        sfg[i] = sfg_sum[:, i * LANES : (i + 1) * LANES]
    send(12, sfg.at[1 - c], sfg_sib, sibling)
    gram_sum = None
    for tile in tiles:
        pad = jnp.zeros((LANES - RANK, tile.shape[1]), F32)
        term = dot6(rows3(tile), split3(jnp.concatenate([tile, pad], axis=0)), NT)
        gram_sum = term if gram_sum is None else gram_sum + term
    packed = gram_sum[0:8]
    for i in range(1, 4):
        packed = packed + pltpu.roll(gram_sum[8 * i : 8 * i + 8], RANK * i, 1)
    gram_own[...] = packed
    send(22, gram_own, gram_sib, sibling)

    received(12, sfg_sib)
    reduce_first(13, sfg[c] + sfg_sib[...], msg_g, z1_g, x1_g)
    received(22, gram_sib)
    gram_pair[...] = gram_own[...] + gram_sib[...]
    gram_all[t] = gram_pair[...]
    for device in xy_peers:
        send(23, gram_pair, gram_all.at[t], device)

    reduce_third(2, z2_d, x2_d, sd)

    hi, mid, lo = split3(sd[c])
    stacked = jnp.concatenate(
        [
            jnp.concatenate([hi, hi], axis=1),
            jnp.concatenate([mid, mid], axis=1),
            jnp.concatenate([lo, jnp.zeros_like(lo)], axis=1),
        ],
        axis=0,
    )

    def product(half):
        for i in range(0, HALF, 2):
            n = min(2, HALF - i)
            cols = pl.ds(pl.multiple_of((half * HALF + i) * LANES, LANES), n * LANES)
            a = dot(stacked, md[0 : 2 * d_half, cols], NN)
            small = dot(hi, md[2 * d_half :, cols], NN) + a[2 * RANK :]
            term = a[:RANK] + (a[RANK : 2 * RANK] + small)
            for k in range(n):
                put_tile(sfd, half, i + k, term[:, k * LANES : (k + 1) * LANES])

    product(1 - c)
    send(9, sfd.at[1 - c], sfd_sib, sibling)
    product(c)

    received(9, sfd_sib)
    scatter(11, sfd, sfd_sib, sfd_half, rs_d)

    received(6, sd.at[1 - c])
    sketch_d = jnp.concatenate([sd[0], sd[1]], axis=1)
    pad = jnp.zeros((LANES - RANK, BLOCK), F32)
    lower_d, upper_d, inv_d = eliminate(dot6(rows3(sketch_d), split3(jnp.concatenate([sketch_d, pad], axis=0)), NT))
    solved = dot(left_lanes(lower_d), right_six(sketch_d), NN) * (inv_d * (1.0 / 16.0))
    left_d[...] = jnp.transpose(left_six(dot(left_lanes(upper_d), right_six(solved), NN)))

    reduce_second(13, z1_g, x1_g, mid_g, z2_g, x2_g)
    send(10, sg.at[c], sg.at[c], sibling)

    gather(18, 11, rs_d, own_d, co_d)

    received(23, gram_all.at[pl.ds(0, XY - 1)])
    gram_packed = total(gram_all, XY)
    lane = lax.broadcasted_iota(jnp.int32, (8, LANES), 1)
    gram_g = jnp.concatenate(
        [jnp.where(lane < RANK, gram_packed if i == 0 else pltpu.roll(gram_packed, LANES - RANK * i, 1), 0.0) for i in range(4)],
        axis=0,
    )
    lower_g, _, inv_g = eliminate(gram_g)
    lower_g = left_lanes(lower_g)
    received(10, sg.at[1 - c])
    for i in range(HALF):
        tile = jnp.concatenate([tile_of(sg, j // HALF, j % HALF) for j in (2 * i, 2 * i + 1)], axis=1)
        left_g[pl.ds(i * BLOCK, BLOCK), :] = jnp.transpose(left_six(dot(lower_g, right_six(tile), NN)))

    reduce_third(13, z2_g, x2_g, sum_g)
    gathered(18, co_d)
    send(19, co_d.at[c], co_d.at[c], sibling)
    received(17, sum_g.at[1 - c])
    coeff = dot(lower_g, right_six(jnp.concatenate([sum_g[0], sum_g[1]], axis=1)), NN) * (inv_g * (1.0 / 16.0))
    right_g[...] = right_six(coeff)
    received(19, co_d.at[1 - c])
    coeff_d[...] = co_d[...]

    sent(0, sd_sib)
    sent(1, sg_sib)
    sent(20, md_in)
    sent(21, mg_in)
    sent(9, sfd_sib)
    sent(12, sfg_sib)
    sent(22, gram_sib)
    sent(23, gram_all.at[pl.ds(0, XY - 1)])
    sent(10, sg_sib)
    sent(19, sg_sib)
    for base, z1, x1, z2, x2, full in (
        (2, z1_d, x1_d, z2_d, x2_d, sd),
        (13, z1_g, x1_g, z2_g, x2_g, sum_g),
    ):
        sent(base, z1.at[pl.ds(0, Z - 1)])
        sent(base + 1, x1.at[pl.ds(0, XY - 1)])
        sent(base + 2, z2.at[pl.ds(0, Z - 1)])
        sent(base + 3, x2.at[pl.ds(0, XY - 1)])
        sent(base + 4, full.at[0])
    for stage, rs in ((7, rs_g), (8, rs_g), (11, rs_d), (18, rs_d)):
        sent(stage, rs.at[pl.ds(0, Z - 1)])


def finish_kernel(full_g, full_d, left_g, right_g, left_d, coeff_d, ug_hbm, ng_hbm, ud_hbm, nd_hbm, ug, ng, ud, nd, sem):
    copies = []

    def store(src, dst):
        copies.append(pltpu.make_async_copy(src, dst, sem.at[len(copies)]))
        copies[-1].start()

    for b in range(full_g.shape[0] // BLOCK):
        part = (pl.ds(b * BLOCK, BLOCK), slice(None))
        update = dot(left_g[part], right_g[...], NN)
        ug[part] = update
        ng[part] = full_g[part] - update
        store(ug.at[part], ug_hbm.at[part])
        store(ng.at[part], ng_hbm.at[part])
        part = (slice(None), pl.ds(b * BLOCK, BLOCK))
        right = right_six(jnp.concatenate([tile_of(coeff_d, j // HALF, j % HALF) for j in (2 * b, 2 * b + 1)], axis=1))
        update = dot(left_d[...], right, NN)
        ud[part] = update
        nd[part] = full_d[part] - update
        store(ud.at[part], ud_hbm.at[part])
        store(nd.at[part], nd_hbm.at[part])
    for copy in copies:
        copy.wait()


def local(grad_gate, error_gate, query_gate, grad_down, error_down, query_down):
    gg, eg, gd, ed = grad_gate[0], error_gate[0], grad_down[0], error_down[0]
    ff, rows = gg.shape
    vmem = pltpu.VMEM
    tile = (RANK, LANES)
    half = (Z, HALF * CHUNK, LANES)
    chunk, both = vmem(half[1:], F32), vmem((2, *half), F32)

    def stack(n, r=RANK):
        return vmem((n, r, LANES), F32)

    def reduce_buffers():
        return [vmem(tile, F32), stack(Z, 16), stack(XY, 16), vmem(tile, F32), stack(Z, 16), stack(XY, 16), stack(2)]

    scratch = (
        [vmem((ff, rows), BF16), vmem((ff, rows), F32), vmem((RANK, rows), F32)]
        + [vmem((rows, ff), BF16), vmem((rows, ff), F32), vmem((RANK, ff), F32)]
        + [vmem((ff // 2, rows), F32), vmem((rows // 2, ff), F32), vmem((3, ff // 2, rows), BF16), vmem((3 * rows // 2, ff), BF16)]
        + [both, vmem(half, F32), vmem(half, F32), vmem(half, F32), both]
        + [stack(2), vmem(tile, F32), vmem((8, LANES), F32), vmem((8, LANES), F32), vmem((8, LANES), F32), stack(XY, 8)] + reduce_buffers()
        + [stack(2), vmem(tile, F32)] + reduce_buffers()
        + [both, vmem(half, F32), vmem(half, F32), vmem(half, F32), chunk, chunk, both]
        + [pltpu.SemaphoreType.DMA((6,)), pltpu.SemaphoreType.DMA((24,)), pltpu.SemaphoreType.DMA((24,))]
    )
    whole = pl.BlockSpec(memory_space=pltpu.VMEM)
    gate_shape, down_shape = (ff, rows), (rows, ff)
    shapes = [
        (gate_shape, F32), (down_shape, F32), ((ff, 6 * RANK), BF16), ((6 * RANK, rows), BF16),
        ((rows, 6 * RANK), BF16), ((2, *half), F32),
    ]
    inputs = [pltpu.with_memory_space_constraint(a, pltpu.HBM) for a in (gg, eg, query_gate, gd, ed, query_down)]
    middle = pl.pallas_call(
        exchange_kernel,
        out_shape=[pltpu.VMEM(shape, dtype) for shape, dtype in shapes],
        in_specs=[pl.BlockSpec(memory_space=pltpu.HBM)] * 6,
        out_specs=[whole] * len(shapes),
        scratch_shapes=scratch,
        compiler_params=pltpu.CompilerParams(collective_id=0, has_side_effects=True, vmem_limit_bytes=32 * 2**20),
    )(*inputs)

    outs = [gate_shape, gate_shape, down_shape, down_shape]
    ug, ng, ud, nd = pl.pallas_call(
        finish_kernel,
        out_shape=[jax.ShapeDtypeStruct(shape, F32) for shape in outs],
        in_specs=[whole] * len(shapes),
        out_specs=[pl.BlockSpec(memory_space=pl.ANY)] * 4,
        scratch_shapes=[vmem(shape, F32) for shape in outs] + [pltpu.SemaphoreType.DMA((4 * (ff // BLOCK),))],
        compiler_params=pltpu.CompilerParams(vmem_limit_bytes=32 * 2**20),
    )(*middle)
    return ug, ng[None], ud, nd[None]


def solution(mesh):
    in_specs = (
        P("dp", "tensor", None),
        P("dp", "tensor", None),
        P(),
        P("dp", None, "tensor"),
        P("dp", None, "tensor"),
        P(None, "tensor"),
    )
    out_specs = (
        P("tensor", None),
        P("dp", "tensor", None),
        P(None, "tensor"),
        P("dp", None, "tensor"),
    )
    return jax.shard_map(local, mesh=mesh, in_specs=in_specs, out_specs=out_specs, check_vma=False)
```

```python
import functools

import jax
import jax.numpy as jnp
from jax import lax
from jax.experimental import pallas as pl
from jax.experimental.pallas import tpu as pltpu
from jax.sharding import PartitionSpec as P

MESH = pl.DeviceIdType.MESH
F32, BF16 = jnp.float32, jnp.bfloat16
NN = (((1,), (0,)), ((), ()))
NT = (((1,), (1,)), ((), ()))
TN = (((0,), (0,)), ((), ()))
LANES = 128
BLOCK = 256
RANK = 32
Z, XY = 8, 16
HALF = 7
CHUNK = 4
SPREAD = 16
Z_ORDER = (4, 3, 5, 2, 6, 1, 7)
XY_ORDER = sorted(
    ((dx, dy) for dx in range(4) for dy in range(4) if dx or dy),
    key=lambda o: -(min(o[0], 4 - o[0]) + min(o[1], 4 - o[1])),
)


def split3(x):
    hi = x.astype(BF16)
    rest = x - hi.astype(F32)
    mid = rest.astype(BF16)
    return hi, mid, (rest - mid.astype(F32)).astype(BF16)


def rows3(x):
    return jnp.concatenate(split3(x), axis=0)


def dot(a, b, dims):
    return lax.dot_general(a, b, dims, preferred_element_type=F32)


def dot6(left3, right, dims):
    hi, mid, lo = right
    a = dot(left3, hi, dims)
    b = dot(left3[: 2 * RANK], mid, dims)
    c = dot(left3[:RANK], lo, dims)
    small = a[2 * RANK :] + b[RANK:] + c
    return a[:RANK] + ((a[RANK : 2 * RANK] + b[:RANK]) + small)


def tile_of(ref, half, i):
    return jnp.concatenate([ref[half, k, CHUNK * i : CHUNK * (i + 1)] for k in range(Z)], axis=0)


def put_tile(ref, half, i, tile):
    for k in range(Z):
        ref[half, k, CHUNK * i : CHUNK * (i + 1)] = tile[k * CHUNK : (k + 1) * CHUNK]


def total(ref, n):
    out = ref[0]
    for i in range(1, n):
        out = out + ref[i]
    return out


def eliminate(gram):
    rows = lax.broadcasted_iota(jnp.int32, (RANK, LANES), 0)
    lanes = lax.broadcasted_iota(jnp.int32, (RANK, LANES), 1)
    a = gram + (lanes == rows + RANK).astype(F32)
    for first in range(0, RANK, SPREAD):
        columns = [jnp.broadcast_to(a[:, k : k + 1], (RANK, LANES)) for k in range(first, first + SPREAD)]
        for i, column in enumerate(columns):
            k = first + i
            factor = jnp.where(rows > k, column, 0.0) * (1.0 / column[k : k + 1])
            for later in range(i + 1, SPREAD):
                columns[later] = columns[later] - factor * columns[later][k : k + 1]
            a = a - factor * a[k : k + 1]
    pivots = jnp.sum(jnp.where(lanes == rows, a, 0.0), axis=1, keepdims=True)
    return a[:, RANK : 2 * RANK], jnp.transpose(a)[RANK : 2 * RANK], 1.0 / pivots


def left_six(x):
    hi, mid, lo = split3(x)
    return jnp.concatenate([hi, hi, mid, hi, lo, mid], axis=0)


def left_lanes(x):
    hi, mid, lo = split3(x)
    return jnp.concatenate([hi, hi, mid, hi, lo, mid], axis=1)


def right_six(x):
    hi, mid, lo = split3(x)
    return jnp.concatenate([hi, mid, hi, lo, hi, mid], axis=0)


def exchange_kernel(
    gg_hbm, eg_hbm, qg_hbm, gd_hbm, ed_hbm, qd_hbm,
    full_g, full_d, left_g, right_g, left_d, coeff_d,
    gg, eg, qg, gd, ed, qd, mg_in, md_in, mg, md,
    sg_part, sg_sib, sg_half, rs_g, sg,
    sfg, sfg_sib, gram_own, gram_sib, gram_pair, gram_all, msg_g, z1_g, x1_g, mid_g, z2_g, x2_g, sum_g,
    sd_part, sd_sib, msg_d, z1_d, x1_d, mid_d, z2_d, x2_d, sd,
    sfd, sfd_sib, sfd_half, rs_d, own_g, own_d,
    load_sem, send_sem, recv_sem,
):
    dp, t = lax.axis_index("dp"), lax.axis_index("tensor")
    z, c = dp // 2, dp % 2
    x, y = t // 4, t % 4
    sibling = (dp + 1 - 2 * c, t)
    z_peers = [(lax.rem(z + i, Z), (2 * lax.rem(z + i, Z) + c, t)) for i in Z_ORDER]
    xy_peers = [(dp, lax.rem(x + dx, 4) * 4 + lax.rem(y + dy, 4)) for dx, dy in XY_ORDER]

    barrier = pltpu.get_barrier_semaphore()
    for device in [sibling] + [d for _, d in z_peers] + xy_peers:
        pl.semaphore_signal(barrier, inc=1, device_id=device, device_id_type=MESH)

    loads = [
        pltpu.make_async_copy(src, dst, load_sem.at[i])
        for i, (src, dst) in enumerate(
            ((qd_hbm, qd), (gd_hbm, gd), (ed_hbm, ed), (qg_hbm, qg), (gg_hbm, gg), (eg_hbm, eg))
        )
    ]
    for load in loads:
        load.start()

    def send(stage, src, dst, device):
        pltpu.make_async_remote_copy(
            src_ref=src, dst_ref=dst, send_sem=send_sem.at[stage], recv_sem=recv_sem.at[stage],
            device_id=device, device_id_type=MESH,
        ).start()

    def received(stage, ref):
        pltpu.make_async_copy(ref, ref, recv_sem.at[stage]).wait()

    def sent(stage, ref):
        pltpu.make_async_copy(ref, ref, send_sem.at[stage]).wait()

    blocks = gg.shape[0] // BLOCK
    g_half, d_half = mg_in.shape[0], md_in.shape[0]
    for load in loads[:3]:
        load.wait()
    sd_sum = None
    for b in range(blocks):
        cols = pl.ds(b * BLOCK, BLOCK)
        block = gd[:, cols].astype(F32) + ed[:, cols]
        full_d[:, cols] = block
        term = dot6(rows3(qd[:, cols]), split3(block), NT)
        sd_sum = term if sd_sum is None else sd_sum + term
    sd_part[0] = sd_sum[:, :LANES]
    sd_part[1] = sd_sum[:, LANES:]
    for load in loads[3:]:
        load.wait()
    qg3 = rows3(qg[...])
    for b in range(blocks):
        rows = pl.ds(b * BLOCK, BLOCK)
        block = gg[rows, :].astype(F32) + eg[rows, :]
        full_g[rows, :] = block
        term = dot6(qg3, split3(block), NT)
        for j, tile in ((2 * b, term[:, :LANES]), (2 * b + 1, term[:, LANES:])):
            put_tile(sg_part, j // HALF, j % HALF, tile)

    pl.semaphore_wait(barrier, 1 + len(z_peers) + len(xy_peers))

    send(1, sg_part.at[1 - c], sg_sib, sibling)
    send(0, sd_part.at[1 - c], sd_sib, sibling)

    def reduce_first(base, value, msg, z1, x1):
        msg[...] = value
        z1[z] = msg[0:16]
        high = msg.at[pl.ds(16, msg.shape[0] - 16)]
        x1[t] = high[...]
        for device in xy_peers:
            send(base + 1, high, x1.at[t], device)
        for _, device in z_peers:
            send(base, msg.at[pl.ds(0, 16)], z1.at[z], device)

    def reduce_second(base, z1, x1, mid, z2, x2):
        received(base, z1.at[pl.ds(0, Z - 1)])
        low = total(z1, Z)
        mid[0:16] = low
        x2[t] = low
        for device in xy_peers:
            send(base + 3, mid.at[pl.ds(0, 16)], x2.at[t], device)
        received(base + 1, x1.at[pl.ds(0, XY - 1)])
        high = total(x1, XY)
        mid[16:32] = high
        z2[z] = high
        for _, device in z_peers:
            send(base + 2, mid.at[pl.ds(16, 16)], z2.at[z], device)

    def reduce_third(base, z2, x2, full):
        received(base + 2, z2.at[pl.ds(0, Z - 1)])
        received(base + 3, x2.at[pl.ds(0, XY - 1)])
        full[c, 0:16] = total(x2, XY)
        full[c, 16:32] = total(z2, Z)
        send(base + 4, full.at[c], full.at[c], sibling)

    def scatter(stage, part, sib, half, rs):
        for k in range(Z):
            half[k] = part[c, k] + sib[k]
        for peer, device in z_peers:
            send(stage, half.at[peer], rs.at[z], device)
        rs[z] = half[z]

    def gather(stage, rs_stage, rs, own, dst):
        received(rs_stage, rs.at[pl.ds(0, Z - 1)])
        own[...] = total(rs, Z)
        for _, device in z_peers:
            send(stage, own, dst.at[c, z], device)
        dst[c, z] = own[...]

    def gathered(stage, dst):
        received(stage, dst.at[c, pl.ds(0, Z - 1)])

    received(1, sg_sib)
    scatter(7, sg_part, sg_sib, sg_half, rs_g)
    received(0, sd_sib)
    reduce_first(2, sd_part[c] + sd_sib[...], msg_d, z1_d, x1_d)
    send(20, full_d.at[pl.ds(pl.multiple_of((1 - c) * d_half, LANES), d_half)], md_in, sibling)
    send(21, full_g.at[pl.ds(pl.multiple_of((1 - c) * g_half, LANES), g_half)], mg_in, sibling)

    received(20, md_in)
    for b in range(blocks):
        cols = pl.ds(b * BLOCK, BLOCK)
        block = full_d[pl.ds(pl.multiple_of(c * d_half, LANES), d_half), cols] + md_in[:, cols]
        hi, mid, lo = split3(block)
        md[0:d_half, cols] = hi
        md[d_half : 2 * d_half, cols] = mid
        md[2 * d_half :, cols] = lo
    received(21, mg_in)
    for b in range(HALF):
        parts = split3(full_g[pl.ds(pl.multiple_of(c * g_half + b * LANES, LANES), LANES), :] + mg_in[pl.ds(b * LANES, LANES), :])
        for i in range(3):
            mg[i, pl.ds(b * LANES, LANES), :] = parts[i]

    gather(8, 7, rs_g, own_g, sg)

    reduce_second(2, z1_d, x1_d, mid_d, z2_d, x2_d)

    gathered(8, sg)
    tiles = [jnp.concatenate([tile_of(sg, c, i) for i in range(b, min(b + 2, HALF))], axis=1) for b in range(0, HALF, 2)]
    sfg_sum = None
    for b, tile in enumerate(tiles):
        rows = pl.ds(b * BLOCK, tile.shape[1])
        term = dot6(rows3(tile), [mg[i, rows, :] for i in range(3)], NN)
        sfg_sum = term if sfg_sum is None else sfg_sum + term
    for i in range(2):
        sfg[i] = sfg_sum[:, i * LANES : (i + 1) * LANES]
    send(12, sfg.at[1 - c], sfg_sib, sibling)
    gram_sum = None
    for tile in tiles:
        pad = jnp.zeros((LANES - RANK, tile.shape[1]), F32)
        term = dot6(rows3(tile), split3(jnp.concatenate([tile, pad], axis=0)), NT)
        gram_sum = term if gram_sum is None else gram_sum + term
    packed = gram_sum[0:8]
    for i in range(1, 4):
        packed = packed + pltpu.roll(gram_sum[8 * i : 8 * i + 8], RANK * i, 1)
    gram_own[...] = packed
    send(22, gram_own, gram_sib, sibling)

    received(12, sfg_sib)
    reduce_first(13, sfg[c] + sfg_sib[...], msg_g, z1_g, x1_g)
    received(22, gram_sib)
    gram_pair[...] = gram_own[...] + gram_sib[...]
    gram_all[t] = gram_pair[...]
    for device in xy_peers:
        send(23, gram_pair, gram_all.at[t], device)

    reduce_third(2, z2_d, x2_d, sd)

    hi, mid, lo = split3(sd[c])
    stacked = jnp.concatenate(
        [
            jnp.concatenate([hi, hi], axis=1),
            jnp.concatenate([mid, mid], axis=1),
            jnp.concatenate([lo, jnp.zeros_like(lo)], axis=1),
        ],
        axis=0,
    )

    def product(half):
        for i in range(0, HALF, 2):
            n = min(2, HALF - i)
            cols = pl.ds(pl.multiple_of((half * HALF + i) * LANES, LANES), n * LANES)
            a = dot(stacked, md[0 : 2 * d_half, cols], NN)
            small = dot(hi, md[2 * d_half :, cols], NN) + a[2 * RANK :]
            term = a[:RANK] + (a[RANK : 2 * RANK] + small)
            for k in range(n):
                put_tile(sfd, half, i + k, term[:, k * LANES : (k + 1) * LANES])

    product(1 - c)
    send(9, sfd.at[1 - c], sfd_sib, sibling)
    product(c)

    received(9, sfd_sib)
    scatter(11, sfd, sfd_sib, sfd_half, rs_d)

    received(6, sd.at[1 - c])
    sketch_d = jnp.concatenate([sd[0], sd[1]], axis=1)
    pad = jnp.zeros((LANES - RANK, BLOCK), F32)
    lower_d, upper_d, inv_d = eliminate(dot6(rows3(sketch_d), split3(jnp.concatenate([sketch_d, pad], axis=0)), NT))
    solved = dot(left_lanes(lower_d), right_six(sketch_d), NN) * (inv_d * (1.0 / 16.0))
    left_d[...] = jnp.transpose(left_six(dot(left_lanes(upper_d), right_six(solved), NN)))

    reduce_second(13, z1_g, x1_g, mid_g, z2_g, x2_g)
    send(10, sg.at[c], sg.at[c], sibling)

    gather(18, 11, rs_d, own_d, coeff_d)

    received(23, gram_all.at[pl.ds(0, XY - 1)])
    gram_packed = total(gram_all, XY)
    lane = lax.broadcasted_iota(jnp.int32, (8, LANES), 1)
    gram_g = jnp.concatenate(
        [jnp.where(lane < RANK, gram_packed if i == 0 else pltpu.roll(gram_packed, LANES - RANK * i, 1), 0.0) for i in range(4)],
        axis=0,
    )
    lower_g, _, inv_g = eliminate(gram_g)
    lower_g = left_lanes(lower_g)
    received(10, sg.at[1 - c])
    for i in range(HALF):
        tile = jnp.concatenate([tile_of(sg, j // HALF, j % HALF) for j in (2 * i, 2 * i + 1)], axis=1)
        left_g[pl.ds(i * BLOCK, BLOCK), :] = jnp.transpose(left_six(dot(lower_g, right_six(tile), NN)))

    reduce_third(13, z2_g, x2_g, sum_g)
    gathered(18, coeff_d)
    send(19, coeff_d.at[c], coeff_d.at[c], sibling)
    received(17, sum_g.at[1 - c])
    coeff = dot(lower_g, right_six(jnp.concatenate([sum_g[0], sum_g[1]], axis=1)), NN) * (inv_g * (1.0 / 16.0))
    right_g[...] = right_six(coeff)
    received(19, coeff_d.at[1 - c])

    sent(0, sd_sib)
    sent(1, sg_sib)
    sent(20, md_in)
    sent(21, mg_in)
    sent(9, sfd_sib)
    sent(12, sfg_sib)
    sent(22, gram_sib)
    sent(23, gram_all.at[pl.ds(0, XY - 1)])
    sent(10, sg_sib)
    sent(19, sg_sib)
    for base, z1, x1, z2, x2, full in (
        (2, z1_d, x1_d, z2_d, x2_d, sd),
        (13, z1_g, x1_g, z2_g, x2_g, sum_g),
    ):
        sent(base, z1.at[pl.ds(0, Z - 1)])
        sent(base + 1, x1.at[pl.ds(0, XY - 1)])
        sent(base + 2, z2.at[pl.ds(0, Z - 1)])
        sent(base + 3, x2.at[pl.ds(0, XY - 1)])
        sent(base + 4, full.at[0])
    for stage, rs in ((7, rs_g), (8, rs_g), (11, rs_d), (18, rs_d)):
        sent(stage, rs.at[pl.ds(0, Z - 1)])


def finish_kernel(full_g, full_d, left_g, right_g, left_d, coeff_d, ug_hbm, ng_hbm, ud_hbm, nd_hbm, ug, ng, ud, nd, sem):
    copies = []

    def store(src, dst):
        copies.append(pltpu.make_async_copy(src, dst, sem.at[len(copies)]))
        copies[-1].start()

    for b in range(full_g.shape[0] // BLOCK):
        part = (pl.ds(b * BLOCK, BLOCK), slice(None))
        update = dot(left_g[part], right_g[...], NN)
        ug[part] = update
        ng[part] = full_g[part] - update
        store(ug.at[part], ug_hbm.at[part])
        store(ng.at[part], ng_hbm.at[part])
        part = (slice(None), pl.ds(b * BLOCK, BLOCK))
        right = right_six(jnp.concatenate([tile_of(coeff_d, j // HALF, j % HALF) for j in (2 * b, 2 * b + 1)], axis=1))
        update = dot(left_d[...], right, NN)
        ud[part] = update
        nd[part] = full_d[part] - update
        store(ud.at[part], ud_hbm.at[part])
        store(nd.at[part], nd_hbm.at[part])
    for copy in copies:
        copy.wait()


def local(grad_gate, error_gate, query_gate, grad_down, error_down, query_down):
    gg, eg, gd, ed = grad_gate[0], error_gate[0], grad_down[0], error_down[0]
    ff, rows = gg.shape
    vmem = pltpu.VMEM
    tile = (RANK, LANES)
    half = (Z, HALF * CHUNK, LANES)
    chunk, both = vmem(half[1:], F32), vmem((2, *half), F32)

    def stack(n, r=RANK):
        return vmem((n, r, LANES), F32)

    def reduce_buffers():
        return [vmem(tile, F32), stack(Z, 16), stack(XY, 16), vmem(tile, F32), stack(Z, 16), stack(XY, 16), stack(2)]

    scratch = (
        [vmem((ff, rows), BF16), vmem((ff, rows), F32), vmem((RANK, rows), F32)]
        + [vmem((rows, ff), BF16), vmem((rows, ff), F32), vmem((RANK, ff), F32)]
        + [vmem((ff // 2, rows), F32), vmem((rows // 2, ff), F32), vmem((3, ff // 2, rows), BF16), vmem((3 * rows // 2, ff), BF16)]
        + [both, vmem(half, F32), vmem(half, F32), vmem(half, F32), both]
        + [stack(2), vmem(tile, F32), vmem((8, LANES), F32), vmem((8, LANES), F32), vmem((8, LANES), F32), stack(XY, 8)] + reduce_buffers()
        + [stack(2), vmem(tile, F32)] + reduce_buffers()
        + [both, vmem(half, F32), vmem(half, F32), vmem(half, F32), chunk, chunk]
        + [pltpu.SemaphoreType.DMA((6,)), pltpu.SemaphoreType.DMA((24,)), pltpu.SemaphoreType.DMA((24,))]
    )
    whole = pl.BlockSpec(memory_space=pltpu.VMEM)
    gate_shape, down_shape = (ff, rows), (rows, ff)
    shapes = [
        (gate_shape, F32), (down_shape, F32), ((ff, 6 * RANK), BF16), ((6 * RANK, rows), BF16),
        ((rows, 6 * RANK), BF16), ((2, *half), F32),
    ]
    inputs = [pltpu.with_memory_space_constraint(a, pltpu.HBM) for a in (gg, eg, query_gate, gd, ed, query_down)]
    middle = pl.pallas_call(
        exchange_kernel,
        out_shape=[pltpu.VMEM(shape, dtype) for shape, dtype in shapes],
        in_specs=[pl.BlockSpec(memory_space=pltpu.HBM)] * 6,
        out_specs=[whole] * len(shapes),
        scratch_shapes=scratch,
        compiler_params=pltpu.CompilerParams(collective_id=0, has_side_effects=True, vmem_limit_bytes=32 * 2**20),
    )(*inputs)

    outs = [gate_shape, gate_shape, down_shape, down_shape]
    ug, ng, ud, nd = pl.pallas_call(
        finish_kernel,
        out_shape=[jax.ShapeDtypeStruct(shape, F32) for shape in outs],
        in_specs=[whole] * len(shapes),
        out_specs=[pl.BlockSpec(memory_space=pl.ANY)] * 4,
        scratch_shapes=[vmem(shape, F32) for shape in outs] + [pltpu.SemaphoreType.DMA((4 * (ff // BLOCK),))],
        compiler_params=pltpu.CompilerParams(vmem_limit_bytes=32 * 2**20),
    )(*middle)
    return ug, ng[None], ud, nd[None]


def solution(mesh):
    in_specs = (
        P("dp", "tensor", None),
        P("dp", "tensor", None),
        P(),
        P("dp", None, "tensor"),
        P("dp", None, "tensor"),
        P(None, "tensor"),
    )
    out_specs = (
        P("tensor", None),
        P("dp", "tensor", None),
        P(None, "tensor"),
        P("dp", None, "tensor"),
    )
    return jax.shard_map(local, mesh=mesh, in_specs=in_specs, out_specs=out_specs, check_vma=False)
```
